256 devices in a mesh: shard: 16 (over x_lo, z), dp: 8 (over y, x_hi), buffer: 2 (over core).
Axes of the slice: x: 4 (x_hi: 2, x_lo: 2; x = x_hi * 2 + x_lo), y: 4, z: 8, core: 2. Of those that a mesh axis runs over, the one named last changes fastest.
Arguments:
- query_grad: bfloat16 [4, 128, 14336], P(None, None, 'dp'), may hold values from -6 to 6
- query_act: bfloat16 [4, 128, 8192], P(None, 'dp', 'shard'), may hold values from -6 to 6
- buffer_grad: bfloat16 [8, 128, 14336], P('buffer', None, 'dp'), may hold values from -6 to 6
- buffer_act: bfloat16 [8, 128, 8192], P('buffer', 'dp', 'shard'), may hold values from -6 to 6
- grad_basis: bfloat16 [14336, 14336], P('shard', 'dp'), may hold values from -0.046875 to 0.046875
- act_basis: bfloat16 [8192, 8192], P('dp', 'shard'), may hold values from -0.0625 to 0.0625
- eigenvalues: float32 [14336, 8192], P('shard', 'dp'), may hold values from 0.01 to 10
Outputs:
- scores: float32 [4, 8], P(None, 'buffer')
The draws below stay inside these ranges and needn't reach their ends.
All inputs are finite; a program needn't handle non-finite values.
Results may differ from the reference program's by a relative error of at most 0.033.
Values may be sent and summed in bfloat16 or wider, within the bound.
No kernel may reach another device: no remote copies, remote signals or barrier semaphores. Data moves between devices by JAX's collectives and lax.ppermute only.
A program may use at most 128 MiB of HBM per device.

```python
import math
import jax
import jax.numpy as jnp
from jax import lax

PH = 14336
Q = 8192
T_SIZE = 128
NQ = 4
NB = 8
N_SHARD = 16
N_DP = 8


def levels(key, dims, cuts, least, largest):
    factor_of, own = 1.0, jax.random.fold_in(key, 6)
    for dim, blocks in cuts:
        steps = jnp.exp(jax.random.uniform(jax.random.fold_in(own, dim), (blocks,), jnp.float32, least / len(cuts), largest / len(cuts)))
        factor_of = factor_of * jnp.repeat(steps, dims[dim] // blocks).reshape([-1 if axis == dim else 1 for axis in range(len(dims))])
    return factor_of


def noise(rng, extent, deviation, most, split=(), kind=jnp.bfloat16):
    values = deviation * jax.random.normal(rng, extent, jnp.float32)
    if split:
        values = values * levels(rng, extent, split, -0.22, 0.18)
    return jnp.clip(values, -most, most).astype(kind)


def setup_inputs(seed: int = 0) -> dict:
    key_of = jax.random.split(jax.random.key(seed), 8)
    query_grad = noise(key_of[0], (NQ, T_SIZE, PH), 1.0, 6.0, ((2, 8),))
    query_act = noise(key_of[1], (NQ, T_SIZE, Q), 1.0, 6.0, ((1, 8), (2, 16)))
    buffer_grad = noise(key_of[2], (NB, T_SIZE, PH), 1.0, 6.0, ((0, 2), (2, 8)))
    buffer_act = noise(key_of[3], (NB, T_SIZE, Q), 1.0, 6.0, ((0, 2), (1, 8), (2, 16)))
    grad_basis = noise(key_of[4], (PH, PH), PH ** -0.5, 0.046875, ((0, 16), (1, 8)))
    act_basis = noise(key_of[5], (Q, Q), Q ** -0.5, 0.0625, ((0, 8), (1, 16)))
    eigenvalues = jnp.clip(jnp.exp(math.log(10.0) - 6.9077553 * jax.random.uniform(key_of[6], (PH, Q), jnp.float32) ** levels(key_of[6], (PH, Q), ((0, 16), (1, 8)), -0.2, 0.2)), 0.01, 10.0)
    return dict(query_grad=query_grad, query_act=query_act, buffer_grad=buffer_grad, buffer_act=buffer_act, grad_basis=grad_basis, act_basis=act_basis, eigenvalues=eigenvalues)


DAMPING = 0.1


def rotate(data, basis, blocks):
    width = data.shape[1] // blocks
    total = jnp.zeros((data.shape[0], basis.shape[0]), jnp.float32)
    for index in range(blocks):
        piece = data[:, index * width:(index + 1) * width]
        columns = basis[:, index * width:(index + 1) * width]
        term = lax.dot_general(piece, columns, (((1,), (1,)), ((), ())), preferred_element_type=jnp.float32)
        rounded = lax.optimization_barrier(term.astype(jnp.bfloat16))
        total = total + rounded.astype(jnp.float32)
    return total.astype(jnp.bfloat16)


def reference(query_grad, query_act, buffer_grad, buffer_act, grad_basis, act_basis, eigenvalues):
    grads = jnp.concatenate([query_grad, buffer_grad], 0).reshape((NQ + NB) * T_SIZE, PH)
    acts = jnp.concatenate([query_act, buffer_act], 0).reshape((NQ + NB) * T_SIZE, Q)
    rotated_grad = rotate(grads, grad_basis, N_DP).reshape(NQ + NB, T_SIZE, PH)
    rotated_act = rotate(acts, act_basis, N_SHARD).reshape(NQ + NB, T_SIZE, Q).astype(jnp.float32)
    act_query = rotated_act[:NQ]
    act_buffer = rotated_act[NQ:]
    eblock = PH // N_SHARD

    def one_block(index):
        start = index * eblock
        piece = lax.dynamic_slice_in_dim(rotated_grad, start, eblock, 2).astype(jnp.float32)
        lam = lax.dynamic_slice_in_dim(eigenvalues, start, eblock, 0)
        block_query = jnp.einsum('nte,ntq->neq', piece[:NQ], act_query, precision=lax.Precision.HIGHEST)
        block_buffer = jnp.einsum('nte,ntq->neq', piece[NQ:], act_buffer, precision=lax.Precision.HIGHEST)
        scaled = block_query / (lam + DAMPING)
        return jnp.dot(scaled.reshape(NQ, -1), block_buffer.reshape(NB, -1).T, precision=lax.Precision.HIGHEST)

    partial_scores = lax.map(one_block, jnp.arange(N_SHARD, dtype=jnp.int32))
    norm = 1.0 / (T_SIZE * (float(PH) * float(Q)) ** 0.5)
    return jnp.sum(partial_scores, 0) * norm
```

```python
import jax
import jax.numpy as jnp
from jax import lax
from jax.experimental import pallas as pl
from jax.experimental.pallas import tpu as pltpu
from jax.sharding import PartitionSpec as P

PH = 14336
Q = 8192
T_SIZE = 128
DAMPING = 0.1
NORM = 1.0 / (T_SIZE * (float(PH) * float(Q)) ** 0.5)

F32 = jnp.float32
BF16 = jnp.bfloat16
NT = (((1,), (1,)), ((), ()))


def params(mib):
    return pltpu.CompilerParams(vmem_limit_bytes=mib * 1024 * 1024)


def rotate_grad_kernel(core_ref, qg_ref, bg_ref, basis_ref, qa_ref, ba_ref, out_ref):
    step = pl.program_id(0)
    n_dp, rows, _ = out_ref.shape
    half_rows = (rows - basis_ref.shape[0] // n_dp) // 2
    eigen = basis_ref.shape[0] // n_dp

    def emit(grads):
        part = lax.dot_general(basis_ref[...], grads, NT, preferred_element_type=F32).astype(BF16)
        for d in range(n_dp):
            out_ref[d, :eigen, :] = part[d * eigen:(d + 1) * eigen, :]

    def pack(top, bottom):
        for d in range(n_dp):
            out_ref[d, eigen:eigen + half_rows, :] = top
            out_ref[d, eigen + half_rows:, :] = bottom

    width = out_ref.shape[2]

    @pl.when(step == 0)
    def _():
        emit(qg_ref[...].reshape(width, qg_ref.shape[2]))
        pack(qa_ref[:, :, :width].reshape(half_rows, width), ba_ref[:2, :, :width].reshape(half_rows, width))

    @pl.when(step > 0)
    def _():
        emit(bg_ref[...].reshape(width, bg_ref.shape[2]))

    @pl.when(step == 1)
    def _():
        pack(qa_ref[:, :, width:].reshape(half_rows, width), ba_ref[:2, :, width:].reshape(half_rows, width))

    @pl.when(step == 2)
    def _():
        pack(ba_ref[2:, :, :width].reshape(half_rows, width), ba_ref[2:, :, width:].reshape(half_rows, width))


def rotate_grad(core, query_grad, buffer_grad, basis, query_act, buffer_act, n_dp):
    inner = basis.shape[1]
    outer = basis.shape[0]
    rows = outer // n_dp + 64
    q_in = query_act.shape[2]
    grid_spec = pltpu.PrefetchScalarGridSpec(
        num_scalar_prefetch=1,
        grid=(3,),
        in_specs=[
            pl.BlockSpec((2, T_SIZE, inner), lambda i, c: (c[0], 0, 0)),
            pl.BlockSpec((2, T_SIZE, inner), lambda i, c: (jnp.maximum(i - 1, 0), 0, 0)),
            pl.BlockSpec((outer, inner), lambda i, c: (0, 0)),
            pl.BlockSpec((2, 16, q_in), lambda i, c: (c[0], 0, 0)),
            pl.BlockSpec((4, 16, q_in), lambda i, c: (0, 0, 0)),
        ],
        out_specs=pl.BlockSpec((n_dp, rows, 256), lambda i, c: (0, 0, i)),
    )
    return pl.pallas_call(
        rotate_grad_kernel,
        grid_spec=grid_spec,
        out_shape=jax.ShapeDtypeStruct((n_dp, rows, 768), BF16),
        compiler_params=params(60),
        cost_estimate=pl.CostEstimate(flops=2 * 768 * outer * inner, bytes_accessed=8 * 1024 * 1024, transcendentals=0),
        name="rotate_grad",
    )(core, query_grad, buffer_grad, basis, query_act, buffer_act)


def rotate_act_kernel(recv_ref, basis_ref, grad_ref, out_ref, acts):
    n_dp, rows, _ = recv_ref.shape
    eigen = grad_ref.shape[0]

    @pl.when(pl.program_id(0) == 0)
    def _():
        total = recv_ref[0, :eigen, :].astype(F32)
        for d in range(1, n_dp):
            total = total + recv_ref[d, :eigen, :].astype(F32)
        grad_ref[...] = total.astype(BF16)
        for d in range(n_dp):
            for n in range(6):
                to = n * T_SIZE + d * 16
                if n < 4:
                    start = eigen + n * 16
                    acts[to:to + 16, :] = recv_ref[d, start:start + 16, :512]
                else:
                    start = eigen + (n - 4) * 16
                    acts[to:to + 16, :256] = recv_ref[d, start:start + 16, 512:]
                    acts[to:to + 16, 256:] = recv_ref[d, start + 32:start + 48, 512:]

    out_ref[...] = lax.dot_general(acts[...], basis_ref[...], NT, preferred_element_type=F32).astype(BF16)


def rotate_act(received, basis):
    n_dp, rows, width = received.shape
    outer, inner = basis.shape
    return pl.pallas_call(
        rotate_act_kernel,
        grid=(outer // 256,),
        in_specs=[
            pl.BlockSpec((n_dp, rows, width), lambda i: (0, 0, 0)),
            pl.BlockSpec((256, inner), lambda i: (i, 0)),
        ],
        out_specs=[
            pl.BlockSpec((rows - 64, width), lambda i: (0, 0)),
            pl.BlockSpec((width, 256), lambda i: (0, i)),
        ],
        out_shape=[
            jax.ShapeDtypeStruct((rows - 64, width), BF16),
            jax.ShapeDtypeStruct((width, outer), BF16),
        ],
        scratch_shapes=[pltpu.VMEM((width, inner), BF16)],
        compiler_params=params(40),
        cost_estimate=pl.CostEstimate(flops=2 * width * outer * inner, bytes_accessed=6 * 1024 * 1024, transcendentals=0),
        name="rotate_act",
    )(received, basis)


def add_parts_kernel(parts_ref, out_ref):
    count = parts_ref.shape[0]
    total = parts_ref[0].astype(F32)
    for s in range(1, count):
        total = total + parts_ref[s].astype(F32)
    total = total.astype(BF16)
    for s in range(count):
        out_ref[s] = total


def add_parts(parts):
    count, rows, width = parts.shape
    return pl.pallas_call(
        add_parts_kernel,
        grid=(2,),
        in_specs=[pl.BlockSpec((count, rows, width // 2), lambda i: (0, 0, i))],
        out_specs=pl.BlockSpec((count, rows, width // 2), lambda i: (0, 0, i)),
        out_shape=jax.ShapeDtypeStruct(parts.shape, BF16),
        compiler_params=params(40),
        cost_estimate=pl.CostEstimate(flops=parts.size, bytes_accessed=4 * parts.size, transcendentals=0),
        name="add_parts",
    )(parts)


def pack_grads_kernel(core_ref, own_ref, other_ref, out_ref):
    half = other_ref.shape[1]
    own = own_ref[:, :half]
    other = other_ref[...]
    first = core_ref[0] == 0
    out_ref[:, :half] = jnp.where(first, own, other)
    out_ref[:, half:2 * half] = jnp.where(first, other, own)
    out_ref[:, 2 * half:] = own_ref[:, half:]


def pack_grads(core, own, other):
    rows, width = own.shape
    half = other.shape[1]
    grid_spec = pltpu.PrefetchScalarGridSpec(
        num_scalar_prefetch=1,
        grid=(4,),
        in_specs=[
            pl.BlockSpec((rows // 4, width), lambda i, c: (i, 0)),
            pl.BlockSpec((rows // 4, half), lambda i, c: (i, 0)),
        ],
        out_specs=pl.BlockSpec((rows // 4, width + half), lambda i, c: (i, 0)),
    )
    return pl.pallas_call(
        pack_grads_kernel,
        grid_spec=grid_spec,
        out_shape=jax.ShapeDtypeStruct((rows, width + half), BF16),
        compiler_params=params(40),
        cost_estimate=pl.CostEstimate(flops=4 * 10**9, bytes_accessed=10 * 10**6, transcendentals=0),
        name="pack_grads",
    )(core, own, other)


def query_columns(grads, after):
    rows, width = grads.shape[0], 256
    return pl.pallas_call(
        query_rows_kernel,
        grid=(2,),
        in_specs=[pl.BlockSpec((rows // 2, width), lambda i: (i, 0)), pl.BlockSpec(memory_space=pl.ANY)],
        out_specs=pl.BlockSpec((rows // 2, width), lambda i: (i, 0)),
        out_shape=jax.ShapeDtypeStruct((rows, width), BF16),
        compiler_params=params(40),
        cost_estimate=pl.CostEstimate(flops=0, bytes_accessed=4 * rows * width, transcendentals=0),
        name="query_columns",
    )(grads, after)


def query_rows_kernel(acts_ref, after_ref, out_ref):
    out_ref[...] = acts_ref[...]


def query_rows(acts, after):
    rows, width = 256, acts.shape[1]
    return pl.pallas_call(
        query_rows_kernel,
        grid=(2,),
        in_specs=[pl.BlockSpec((rows // 2, width), lambda i: (i, 0)), pl.BlockSpec(memory_space=pl.ANY)],
        out_specs=pl.BlockSpec((rows // 2, width), lambda i: (i, 0)),
        out_shape=jax.ShapeDtypeStruct((rows, width), BF16),
        compiler_params=params(40),
        cost_estimate=pl.CostEstimate(flops=0, bytes_accessed=4 * rows * width, transcendentals=0),
        name="query_rows",
    )(acts, after)


PIECE = 64


def scores_kernel(core_ref, g_ref, a_ref, ao_ref, eig_ref, out_ref, inverse, left, right, total):
    step = pl.program_id(0)
    eigen = g_ref.shape[0]
    width = a_ref.shape[1]
    inverse[...] = 1.0 / (eig_ref[...] + DAMPING)

    def tile(n, acts):
        return jnp.dot(g_ref[:, n * T_SIZE:(n + 1) * T_SIZE], acts, preferred_element_type=F32)

    def keep(ref, slot, block):
        for c in range(eigen // PIECE):
            ref[slot * PIECE:(slot + 1) * PIECE, c * width:(c + 1) * width] = block[c * PIECE:(c + 1) * PIECE, :]

    first = core_ref[0] == 0
    for i in range(4):
        part = slice((i % 2) * T_SIZE, (i % 2 + 1) * T_SIZE)
        acts = jnp.where(first == (i < 2), a_ref[part, :], ao_ref[part, :])
        keep(left, i, (tile(i, acts) * inverse[...]).astype(BF16))
    for j in range(4):
        keep(right, j, tile(4 + j, a_ref[(2 + j) * T_SIZE:(3 + j) * T_SIZE, :]).astype(BF16))
    product = lax.dot_general(left[...], right[...], NT, preferred_element_type=F32)

    @pl.when(step == 0)
    def _():
        total[...] = product

    @pl.when(step > 0)
    def _():
        total[...] += product

    @pl.when(step == pl.num_programs(0) - 1)
    def _():
        size = total.shape[0]
        row = lax.broadcasted_iota(jnp.int32, (size, size), 0)
        column = lax.broadcasted_iota(jnp.int32, (size, size), 1)
        own = jnp.where(row % PIECE == column % PIECE, total[...], 0.0)
        lane = lax.broadcasted_iota(jnp.int32, (1, size), 1)
        place = lax.broadcasted_iota(jnp.int32, (8, 128), 1)
        result = jnp.zeros((8, 128), F32)
        for i in range(4):
            line = jnp.sum(own[i * PIECE:(i + 1) * PIECE, :], axis=0, keepdims=True)
            for j in range(4):
                value = jnp.sum(jnp.where(lane // PIECE == j, line, 0.0), axis=1, keepdims=True) * NORM
                result = result + jnp.where(place == i * 4 + j, value, 0.0)
        out_ref[...] = result


def tile_scores(core, grads, acts, acts_other, eigenvalues):
    eigen = grads.shape[0]
    rows = acts.shape[0]
    width = eigenvalues.shape[1]
    block = 256
    pieces = eigen // PIECE
    grid_spec = pltpu.PrefetchScalarGridSpec(
        num_scalar_prefetch=1,
        grid=(width // block,),
        in_specs=[
            pl.BlockSpec(grads.shape, lambda i, c: (0, 0)),
            pl.BlockSpec((rows, block), lambda i, c: (0, i)),
            pl.BlockSpec((256, block), lambda i, c: (0, i)),
            pl.BlockSpec((eigen, block), lambda i, c: (0, i)),
        ],
        out_specs=pl.BlockSpec((8, 128), lambda i, c: (0, 0)),
        scratch_shapes=[
            pltpu.VMEM((eigen, block), F32),
            pltpu.VMEM((4 * PIECE, pieces * block), BF16),
            pltpu.VMEM((4 * PIECE, pieces * block), BF16),
            pltpu.VMEM((4 * PIECE, 4 * PIECE), F32),
        ],
    )
    return pl.pallas_call(
        scores_kernel,
        grid_spec=grid_spec,
        out_shape=jax.ShapeDtypeStruct((8, 128), F32),
        compiler_params=params(40),
        cost_estimate=pl.CostEstimate(flops=4 * 8 * T_SIZE * eigen * width, bytes_accessed=8 * 1024 * 1024, transcendentals=0),
        name="tile_scores",
    )(core, grads, acts, acts_other, eigenvalues)


def local(query_grad, query_act, buffer_grad, buffer_act, grad_basis, act_basis, eigenvalues):
    n_dp, n_shard = lax.axis_size("dp"), lax.axis_size("shard")
    core = lax.axis_index("buffer").astype(jnp.int32).reshape(1)
    swap = [(0, 1), (1, 0)]
    sent = rotate_grad(core, query_grad, buffer_grad, grad_basis, query_act, buffer_act, n_dp)
    received = lax.all_to_all(sent, "dp", 0, 0, tiled=True)
    grad_piece, act_part = rotate_act(received, act_basis)
    grads = lax.all_gather(grad_piece, "dp", axis=0, tiled=True)
    parts = lax.all_to_all(act_part.reshape(n_shard, -1, act_part.shape[1]), "shard", 0, 0, tiled=True)
    sums = add_parts(parts)
    grads_other = lax.ppermute(query_columns(grads, sums), "buffer", swap)
    packed = pack_grads(core, grads, grads_other)
    acts = lax.all_to_all(sums, "shard", 0, 0, tiled=True).reshape(act_part.shape)
    acts_other = lax.ppermute(query_rows(acts, packed), "buffer", swap)
    mine = tile_scores(core, packed, acts, acts_other, eigenvalues)
    count = n_dp * n_shard
    every = lax.all_to_all(jnp.broadcast_to(mine[None, :1], (count, 1, 128)), ("shard", "dp"), 0, 0, tiled=True)
    return jnp.sum(every, axis=(0, 1))[:16].reshape(4, 4)


def solution(mesh):
    in_specs = (
        P(None, None, "dp"),
        P(None, "dp", "shard"),
        P("buffer", None, "dp"),
        P("buffer", "dp", "shard"),
        P("shard", "dp"),
        P("dp", "shard"),
        P("shard", "dp"),
    )
    out_specs = P(None, "buffer")
    return jax.shard_map(local, mesh=mesh, in_specs=in_specs, out_specs=out_specs, check_vma=False)
```

```python
import jax
import jax.numpy as jnp
from jax import lax
from jax.experimental import pallas as pl
from jax.experimental.pallas import tpu as pltpu
from jax.sharding import PartitionSpec as P

PH = 14336
Q = 8192
T_SIZE = 128
DAMPING = 0.1
NORM = 1.0 / (T_SIZE * (float(PH) * float(Q)) ** 0.5)

F32 = jnp.float32
BF16 = jnp.bfloat16
NT = (((1,), (1,)), ((), ()))


def params(mib):
    return pltpu.CompilerParams(vmem_limit_bytes=mib * 1024 * 1024)


def pack_acts_kernel(core_ref, qa_ref, ba_ref, out_ref):
    half = qa_ref.shape[0] * qa_ref.shape[1]
    width = qa_ref.shape[2]
    for d in range(out_ref.shape[0]):
        out_ref[d, :half, :] = qa_ref[...].reshape(half, width)
        out_ref[d, half:, :] = ba_ref[...].reshape(2 * half, width)


def pack_acts(core, query_act, buffer_act, copies):
    _, tokens, width = query_act.shape
    grid_spec = pltpu.PrefetchScalarGridSpec(
        num_scalar_prefetch=1,
        grid=(1,),
        in_specs=[
            pl.BlockSpec((2, tokens, width), lambda i, c: (c[0], 0, 0)),
            pl.BlockSpec((4, tokens, width), lambda i, c: (0, 0, 0)),
        ],
        out_specs=pl.BlockSpec((copies, 6 * tokens, width), lambda i, c: (0, 0, 0)),
    )
    return pl.pallas_call(
        pack_acts_kernel,
        grid_spec=grid_spec,
        out_shape=jax.ShapeDtypeStruct((copies, 6 * tokens, width), BF16),
        compiler_params=params(60),
        cost_estimate=pl.CostEstimate(flops=0, bytes_accessed=2 * 1024 * 1024, transcendentals=0),
        name="pack_acts",
    )(core, query_act, buffer_act)


def rotate_grad_kernel(where_ref, qg_ref, bg_ref, basis_ref, *refs):
    outs, part = refs[:-1], refs[-1]
    width = part.shape[1]
    rows = outs[0].shape[0]

    def emit(grads):
        block = grads[...].reshape(width, grads.shape[2])
        part[...] = lax.dot_general(basis_ref[...], block, NT, preferred_element_type=F32).astype(BF16)

    @pl.when(pl.program_id(0) == 0)
    def _():
        emit(qg_ref)

    @pl.when(pl.program_id(0) > 0)
    def _():
        emit(bg_ref)

    for k, out_ref in enumerate(outs):
        start = pl.multiple_of(lax.rem(where_ref[1] + k, len(outs)) * rows, 16)
        out_ref[...] = part[pl.ds(start, rows), :]


def rotate_grad(where, query_grad, buffer_grad, basis, n_y):
    outer, inner = basis.shape
    rows = outer // n_y
    grid_spec = pltpu.PrefetchScalarGridSpec(
        num_scalar_prefetch=1,
        grid=(3,),
        in_specs=[
            pl.BlockSpec((2, T_SIZE, inner), lambda i, c: (c[0], 0, 0)),
            pl.BlockSpec((2, T_SIZE, inner), lambda i, c: (jnp.maximum(i - 1, 0), 0, 0)),
            pl.BlockSpec((outer, inner), lambda i, c: (0, 0)),
        ],
        out_specs=[pl.BlockSpec((rows, 256), lambda i, c: (0, i))] * n_y,
        scratch_shapes=[pltpu.VMEM((outer, 256), BF16)],
    )
    return pl.pallas_call(
        rotate_grad_kernel,
        grid_spec=grid_spec,
        out_shape=[jax.ShapeDtypeStruct((rows, 768), BF16)] * n_y,
        compiler_params=params(60),
        cost_estimate=pl.CostEstimate(flops=2 * 768 * outer * inner, bytes_accessed=8 * 1024 * 1024, transcendentals=0),
        name="rotate_grad",
    )(where, query_grad, buffer_grad, basis)


def add_grads_kernel(where_ref, *refs):
    parts, keep_ref, send_ref = refs[:-3], refs[-3], refs[-2]
    total = refs[-1]
    value = parts[0][...].astype(F32)
    for part in parts[1:]:
        value = value + part[...].astype(F32)
    total[...] = value.astype(BF16)
    rows = keep_ref.shape[0]
    keep_ref[...] = total[pl.ds(pl.multiple_of(where_ref[2] * rows, 16), rows), :]
    send_ref[...] = total[pl.ds(pl.multiple_of((1 - where_ref[2]) * rows, 16), rows), :]


def add_grads(where, parts):
    rows, width = parts[0].shape
    half = jax.ShapeDtypeStruct((rows // 2, width), BF16)
    grid_spec = pltpu.PrefetchScalarGridSpec(
        num_scalar_prefetch=1,
        grid=(1,),
        in_specs=[pl.BlockSpec((rows, width), lambda i, c: (0, 0))] * len(parts),
        out_specs=[pl.BlockSpec((rows // 2, width), lambda i, c: (0, 0))] * 2,
        scratch_shapes=[pltpu.VMEM((rows, width), BF16)],
    )
    return pl.pallas_call(
        add_grads_kernel,
        grid_spec=grid_spec,
        out_shape=[half, half],
        compiler_params=params(40),
        cost_estimate=pl.CostEstimate(flops=4 * rows * width, bytes_accessed=12 * rows * width, transcendentals=0),
        name="add_grads",
    )(where, *parts)


def pair_grads_kernel(where_ref, own_ref, other_ref, out_ref):
    rows = own_ref.shape[0]
    first = where_ref[2] == 0
    out_ref[:rows, :] = jnp.where(first, own_ref[...], other_ref[...])
    out_ref[rows:, :] = jnp.where(first, other_ref[...], own_ref[...])


def pair_grads(where, own, other):
    rows, width = own.shape
    grid_spec = pltpu.PrefetchScalarGridSpec(
        num_scalar_prefetch=1,
        grid=(1,),
        in_specs=[pl.BlockSpec((rows, width), lambda i, c: (0, 0))] * 2,
        out_specs=pl.BlockSpec((2 * rows, width), lambda i, c: (0, 0)),
    )
    return pl.pallas_call(
        pair_grads_kernel,
        grid_spec=grid_spec,
        out_shape=jax.ShapeDtypeStruct((2 * rows, width), BF16),
        compiler_params=params(40),
        cost_estimate=pl.CostEstimate(flops=0, bytes_accessed=8 * rows * width, transcendentals=0),
        name="pair_grads",
    )(where, own, other)


def join_grads_kernel(where_ref, *refs):
    parts, out_ref, query_ref = refs[:-2], refs[-2], refs[-1]
    rows = parts[0].shape[0]
    half = query_ref.shape[1]
    count = len(parts)
    for k, part in enumerate(parts):
        start = pl.multiple_of(lax.rem(where_ref[1] + count - k, count) * rows, 16)
        out_ref[pl.ds(start, rows), :] = part[...]
        query_ref[pl.ds(start, rows), :] = part[:, :half]


def join_grads(where, parts):
    rows, width = parts[0].shape
    full = rows * len(parts)
    grid_spec = pltpu.PrefetchScalarGridSpec(
        num_scalar_prefetch=1,
        grid=(1,),
        in_specs=[pl.BlockSpec((rows, width), lambda i, c: (0, 0))] * len(parts),
        out_specs=[pl.BlockSpec((full, width), lambda i, c: (0, 0)), pl.BlockSpec((full, 256), lambda i, c: (0, 0))],
    )
    return pl.pallas_call(
        join_grads_kernel,
        grid_spec=grid_spec,
        out_shape=[jax.ShapeDtypeStruct((full, width), BF16), jax.ShapeDtypeStruct((full, 256), BF16)],
        compiler_params=params(40),
        cost_estimate=pl.CostEstimate(flops=0, bytes_accessed=5 * full * width, transcendentals=0),
        name="join_grads",
    )(where, *parts)


def rotate_act_kernel(recv_ref, basis_ref, after_ref, out_ref, acts):
    @pl.when(pl.program_id(0) == 0)
    def _():
        for d in range(recv_ref.shape[0]):
            for n in range(6):
                to = n * T_SIZE + d * 16
                acts[to:to + 16, :] = recv_ref[d, n * 16:(n + 1) * 16, :]

    out_ref[...] = lax.dot_general(acts[...], basis_ref[...], NT, preferred_element_type=F32).astype(BF16)


def rotate_act(received, basis, after):
    n_dp, rows, inner = received.shape
    outer = basis.shape[0]
    return pl.pallas_call(
        rotate_act_kernel,
        grid=(outer // 256,),
        in_specs=[
            pl.BlockSpec((n_dp, rows, inner), lambda i: (0, 0, 0)),
            pl.BlockSpec((256, inner), lambda i: (i, 0)),
            pl.BlockSpec(memory_space=pl.ANY),
        ],
        out_specs=pl.BlockSpec((768, 256), lambda i: (0, i)),
        out_shape=jax.ShapeDtypeStruct((768, outer), BF16),
        scratch_shapes=[pltpu.VMEM((768, inner), BF16)],
        compiler_params=params(40),
        cost_estimate=pl.CostEstimate(flops=2 * 768 * outer * inner, bytes_accessed=6 * 1024 * 1024, transcendentals=0),
        name="rotate_act",
    )(received, basis, after)


def add_parts_kernel(parts_ref, keep_ref, came_ref, out_ref, piece_ref):
    count = parts_ref.shape[0]
    total = parts_ref[0].astype(F32)
    for s in range(1, count):
        total = total + parts_ref[s].astype(F32)
    total = total.astype(BF16)
    for s in range(count):
        out_ref[s] = total
    piece_ref[...] = (keep_ref[...].astype(F32) + came_ref[...].astype(F32)).astype(BF16)


def add_parts(parts, keep, came):
    count, rows, width = parts.shape
    high, wide = keep.shape
    return pl.pallas_call(
        add_parts_kernel,
        grid=(2,),
        in_specs=[
            pl.BlockSpec((count, rows, width // 2), lambda i: (0, 0, i)),
            pl.BlockSpec((high, wide // 2), lambda i: (0, i)),
            pl.BlockSpec((high, wide // 2), lambda i: (0, i)),
        ],
        out_specs=[
            pl.BlockSpec((count, rows, width // 2), lambda i: (0, 0, i)),
            pl.BlockSpec((high, wide // 2), lambda i: (0, i)),
        ],
        out_shape=[jax.ShapeDtypeStruct(parts.shape, BF16), jax.ShapeDtypeStruct(keep.shape, BF16)],
        compiler_params=params(40),
        cost_estimate=pl.CostEstimate(flops=parts.size, bytes_accessed=4 * parts.size, transcendentals=0),
        name="add_parts",
    )(parts, keep, came)


def query_rows_kernel(acts_ref, after_ref, out_ref):
    out_ref[...] = acts_ref[...]


def query_rows(acts, after):
    rows, width = 256, acts.shape[1]
    return pl.pallas_call(
        query_rows_kernel,
        grid=(2,),
        in_specs=[pl.BlockSpec((rows // 2, width), lambda i: (i, 0)), pl.BlockSpec(memory_space=pl.ANY)],
        out_specs=pl.BlockSpec((rows // 2, width), lambda i: (i, 0)),
        out_shape=jax.ShapeDtypeStruct((rows, width), BF16),
        compiler_params=params(40),
        cost_estimate=pl.CostEstimate(flops=0, bytes_accessed=4 * rows * width, transcendentals=0),
        name="query_rows",
    )(acts, after)


PIECE = 64


def scores_kernel(core_ref, g_ref, go_ref, a_ref, ao_ref, eig_ref, out_ref, inverse, left, right, total):
    step = pl.program_id(0)
    eigen = g_ref.shape[0]
    width = a_ref.shape[1]
    inverse[...] = 1.0 / (eig_ref[...] + DAMPING)

    def tile(grads, acts, n):
        part = slice(n * T_SIZE, (n + 1) * T_SIZE)
        return jnp.dot(grads[:, part], acts[part, :], preferred_element_type=F32)

    def keep(ref, slot, block):
        for c in range(eigen // PIECE):
            ref[slot * PIECE:(slot + 1) * PIECE, c * width:(c + 1) * width] = block[c * PIECE:(c + 1) * PIECE, :]

    for i in range(2):
        keep(left, i, (tile(g_ref, a_ref, i) * inverse[...]).astype(BF16))
    for j in range(4):
        keep(right, j, tile(g_ref, a_ref, 2 + j).astype(BF16))
    for i in range(2):
        keep(left, 2 + i, (tile(go_ref, ao_ref, i) * inverse[...]).astype(BF16))
    product = lax.dot_general(left[...], right[...], NT, preferred_element_type=F32)

    @pl.when(step == 0)
    def _():
        total[...] = product

    @pl.when(step > 0)
    def _():
        total[...] += product

    @pl.when(step == pl.num_programs(0) - 1)
    def _():
        size = total.shape[0]
        row = lax.broadcasted_iota(jnp.int32, (size, size), 0)
        column = lax.broadcasted_iota(jnp.int32, (size, size), 1)
        own = jnp.where(row % PIECE == column % PIECE, total[...], 0.0)
        lane = lax.broadcasted_iota(jnp.int32, (1, size), 1)
        place = lax.broadcasted_iota(jnp.int32, (8, 128), 1)
        result = jnp.zeros((8, 128), F32)
        for i in range(4):
            line = jnp.sum(own[i * PIECE:(i + 1) * PIECE, :], axis=0, keepdims=True)
            query = (i + 2 * core_ref[0]) % 4
            for j in range(4):
                value = jnp.sum(jnp.where(lane // PIECE == j, line, 0.0), axis=1, keepdims=True) * NORM
                result = result + jnp.where(place == query * 4 + j, value, 0.0)
        out_ref[...] = result


def tile_scores(core, grads, grads_other, acts, acts_other, eigenvalues):
    eigen = grads.shape[0]
    rows = acts.shape[0]
    width = eigenvalues.shape[1]
    block = 256
    pieces = eigen // PIECE
    grid_spec = pltpu.PrefetchScalarGridSpec(
        num_scalar_prefetch=1,
        grid=(width // block,),
        in_specs=[
            pl.BlockSpec(grads.shape, lambda i, c: (0, 0)),
            pl.BlockSpec(grads_other.shape, lambda i, c: (0, 0)),
            pl.BlockSpec((rows, block), lambda i, c: (0, i)),
            pl.BlockSpec((256, block), lambda i, c: (0, i)),
            pl.BlockSpec((eigen, block), lambda i, c: (0, i)),
        ],
        out_specs=pl.BlockSpec((8, 128), lambda i, c: (0, 0)),
        scratch_shapes=[
            pltpu.VMEM((eigen, block), F32),
            pltpu.VMEM((4 * PIECE, pieces * block), BF16),
            pltpu.VMEM((4 * PIECE, pieces * block), BF16),
            pltpu.VMEM((4 * PIECE, 4 * PIECE), F32),
        ],
    )
    return pl.pallas_call(
        scores_kernel,
        grid_spec=grid_spec,
        out_shape=jax.ShapeDtypeStruct((8, 128), F32),
        compiler_params=params(40),
        cost_estimate=pl.CostEstimate(flops=4 * 8 * T_SIZE * eigen * width, bytes_accessed=8 * 1024 * 1024, transcendentals=0),
        name="tile_scores",
    )(core, grads, grads_other, acts, acts_other, eigenvalues)


def local(query_grad, query_act, buffer_grad, buffer_act, grad_basis, act_basis, eigenvalues):
    n_dp, n_shard = lax.axis_size("dp"), lax.axis_size("shard")
    n_y = n_dp // 2
    core = lax.axis_index("buffer").astype(jnp.int32)
    place = lax.axis_index("dp").astype(jnp.int32)
    where = jnp.stack([core, place // 2, place % 2])
    swap = [(0, 1), (1, 0)]
    partner = [(d, d ^ 1) for d in range(n_dp)]

    def along_y(piece, k):
        return lax.ppermute(piece, "dp", [(d, (d + 2 * k) % n_dp) for d in range(n_dp)])

    received = lax.all_to_all(pack_acts(where, query_act, buffer_act, n_dp), "dp", 0, 0, tiled=True)
    blocks = rotate_grad(where, query_grad, buffer_grad, grad_basis, n_y)
    act_part = rotate_act(received, act_basis, blocks[0])
    parts = lax.all_to_all(act_part.reshape(n_shard, -1, act_part.shape[1]), "shard", 0, 0, tiled=True)
    keep, send = add_grads(where, [blocks[0]] + [along_y(blocks[k], k) for k in range(1, n_y)])
    sums, piece = add_parts(parts, keep, lax.ppermute(send, "dp", partner))
    acts = lax.all_to_all(sums, "shard", 0, 0, tiled=True).reshape(act_part.shape)
    pair = pair_grads(where, piece, lax.ppermute(piece, "dp", partner))
    grads, grads_query = join_grads(where, [pair] + [along_y(pair, k) for k in range(1, n_y)])
    grads_other = lax.ppermute(grads_query, "buffer", swap)
    acts_other = lax.ppermute(query_rows(acts, grads_other), "buffer", swap)
    mine = tile_scores(where, grads, grads_other, acts, acts_other, eigenvalues)
    count = n_dp * n_shard
    every = lax.all_to_all(jnp.broadcast_to(mine[None, :1], (count, 1, 128)), ("shard", "dp"), 0, 0, tiled=True)
    return jnp.sum(every, axis=(0, 1))[:16].reshape(4, 4)


def solution(mesh):
    in_specs = (
        P(None, None, "dp"),
        P(None, "dp", "shard"),
        P("buffer", None, "dp"),
        P("buffer", "dp", "shard"),
        P("shard", "dp"),
        P("dp", "shard"),
        P("shard", "dp"),
    )
    out_specs = P(None, "buffer")
    return jax.shard_map(local, mesh=mesh, in_specs=in_specs, out_specs=out_specs, check_vma=False)
```

```python
import jax
import jax.numpy as jnp
from jax import lax
from jax.experimental import pallas as pl
from jax.experimental.pallas import tpu as pltpu
from jax.sharding import PartitionSpec as P

PH = 14336
Q = 8192
T_SIZE = 128
DAMPING = 0.1
NORM = 1.0 / (T_SIZE * (float(PH) * float(Q)) ** 0.5)

F32 = jnp.float32
BF16 = jnp.bfloat16
NT = (((1,), (1,)), ((), ()))


TOKEN = pl.BlockSpec((16, 128), lambda *_: (0, 0))


def params(mib):
    return pltpu.CompilerParams(vmem_limit_bytes=mib * 1024 * 1024)


def pack_acts_kernel(core_ref, qa_ref, ba_ref, out_ref):
    half = qa_ref.shape[0] * qa_ref.shape[1]
    width = qa_ref.shape[2]
    for d in range(out_ref.shape[0]):
        out_ref[d, :half, :] = qa_ref[...].reshape(half, width)
        out_ref[d, half:, :] = ba_ref[...].reshape(2 * half, width)


def pack_acts(core, query_act, buffer_act, copies):
    _, tokens, width = query_act.shape
    grid_spec = pltpu.PrefetchScalarGridSpec(
        num_scalar_prefetch=1,
        grid=(1,),
        in_specs=[
            pl.BlockSpec((2, tokens, width), lambda i, c: (c[0], 0, 0)),
            pl.BlockSpec((4, tokens, width), lambda i, c: (0, 0, 0)),
        ],
        out_specs=pl.BlockSpec((copies, 6 * tokens, width), lambda i, c: (0, 0, 0)),
    )
    return pl.pallas_call(
        pack_acts_kernel,
        grid_spec=grid_spec,
        out_shape=jax.ShapeDtypeStruct((copies, 6 * tokens, width), BF16),
        compiler_params=params(60),
        cost_estimate=pl.CostEstimate(flops=0, bytes_accessed=2 * 1024 * 1024, transcendentals=0),
        name="pack_acts",
    )(core, query_act, buffer_act)


def rotate_grad_kernel(where_ref, qg_ref, bg_ref, basis_ref, *refs):
    outs, part = refs[:-1], refs[-1]
    width = part.shape[1]
    rows = outs[0].shape[0]

    def emit(grads):
        block = grads[...].reshape(width, grads.shape[2])
        part[...] = lax.dot_general(basis_ref[...], block, NT, preferred_element_type=F32).astype(BF16)

    @pl.when(pl.program_id(0) == 0)
    def _():
        emit(qg_ref)

    @pl.when(pl.program_id(0) > 0)
    def _():
        emit(bg_ref)

    for k, out_ref in enumerate(outs):
        start = pl.multiple_of(lax.rem(where_ref[1] + k, len(outs)) * rows, 16)
        out_ref[...] = part[pl.ds(start, rows), :]


def rotate_grad(where, query_grad, buffer_grad, basis, n_y):
    outer, inner = basis.shape
    rows = outer // n_y
    grid_spec = pltpu.PrefetchScalarGridSpec(
        num_scalar_prefetch=1,
        grid=(3,),
        in_specs=[
            pl.BlockSpec((2, T_SIZE, inner), lambda i, c: (c[0], 0, 0)),
            pl.BlockSpec((2, T_SIZE, inner), lambda i, c: (jnp.maximum(i - 1, 0), 0, 0)),
            pl.BlockSpec((outer, inner), lambda i, c: (0, 0)),
        ],
        out_specs=[pl.BlockSpec((rows, 256), lambda i, c: (0, i))] * n_y,
        scratch_shapes=[pltpu.VMEM((outer, 256), BF16)],
    )
    return pl.pallas_call(
        rotate_grad_kernel,
        grid_spec=grid_spec,
        out_shape=[jax.ShapeDtypeStruct((rows, 768), BF16)] * n_y,
        compiler_params=params(60),
        cost_estimate=pl.CostEstimate(flops=2 * 768 * outer * inner, bytes_accessed=8 * 1024 * 1024, transcendentals=0),
        name="rotate_grad",
    )(where, query_grad, buffer_grad, basis)


def add_grads_kernel(where_ref, *refs):
    parts, keep_ref, send_ref = refs[:-3], refs[-3], refs[-2]
    total = refs[-1]
    value = parts[0][...].astype(F32)
    for part in parts[1:]:
        value = value + part[...].astype(F32)
    total[...] = value.astype(BF16)
    rows = keep_ref.shape[0]
    keep_ref[...] = total[pl.ds(pl.multiple_of(where_ref[2] * rows, 16), rows), :]
    send_ref[...] = total[pl.ds(pl.multiple_of((1 - where_ref[2]) * rows, 16), rows), :]


def add_grads(where, parts):
    rows, width = parts[0].shape
    half = jax.ShapeDtypeStruct((rows // 2, width), BF16)
    grid_spec = pltpu.PrefetchScalarGridSpec(
        num_scalar_prefetch=1,
        grid=(1,),
        in_specs=[pl.BlockSpec((rows, width), lambda i, c: (0, 0))] * len(parts),
        out_specs=[pl.BlockSpec((rows // 2, width), lambda i, c: (0, 0))] * 2,
        scratch_shapes=[pltpu.VMEM((rows, width), BF16)],
    )
    return pl.pallas_call(
        add_grads_kernel,
        grid_spec=grid_spec,
        out_shape=[half, half],
        compiler_params=params(40),
        cost_estimate=pl.CostEstimate(flops=4 * rows * width, bytes_accessed=12 * rows * width, transcendentals=0),
        name="add_grads",
    )(where, *parts)


def pair_grads_kernel(where_ref, own_ref, other_ref, out_ref):
    rows = own_ref.shape[0]
    first = where_ref[2] == 0
    out_ref[:rows, :] = jnp.where(first, own_ref[...], other_ref[...])
    out_ref[rows:, :] = jnp.where(first, other_ref[...], own_ref[...])


def pair_grads(where, own, other):
    rows, width = own.shape
    grid_spec = pltpu.PrefetchScalarGridSpec(
        num_scalar_prefetch=1,
        grid=(1,),
        in_specs=[pl.BlockSpec((rows, width), lambda i, c: (0, 0))] * 2,
        out_specs=pl.BlockSpec((2 * rows, width), lambda i, c: (0, 0)),
    )
    return pl.pallas_call(
        pair_grads_kernel,
        grid_spec=grid_spec,
        out_shape=jax.ShapeDtypeStruct((2 * rows, width), BF16),
        compiler_params=params(40),
        cost_estimate=pl.CostEstimate(flops=0, bytes_accessed=8 * rows * width, transcendentals=0),
        name="pair_grads",
    )(where, own, other)


def join_grads_kernel(where_ref, *refs):
    parts, out_ref, query_ref = refs[:-2], refs[-2], refs[-1]
    rows = parts[0].shape[0]
    half = query_ref.shape[1]
    count = len(parts)
    for k, part in enumerate(parts):
        start = pl.multiple_of(lax.rem(where_ref[1] + count - k, count) * rows, 16)
        out_ref[pl.ds(start, rows), :] = part[...]
        query_ref[pl.ds(start, rows), :] = part[:, :half]


def join_grads(where, parts):
    rows, width = parts[0].shape
    full = rows * len(parts)
    grid_spec = pltpu.PrefetchScalarGridSpec(
        num_scalar_prefetch=1,
        grid=(1,),
        in_specs=[pl.BlockSpec((rows, width), lambda i, c: (0, 0))] * len(parts),
        out_specs=[pl.BlockSpec((full, width), lambda i, c: (0, 0)), pl.BlockSpec((full, 256), lambda i, c: (0, 0))],
    )
    return pl.pallas_call(
        join_grads_kernel,
        grid_spec=grid_spec,
        out_shape=[jax.ShapeDtypeStruct((full, width), BF16), jax.ShapeDtypeStruct((full, 256), BF16)],
        compiler_params=params(40),
        cost_estimate=pl.CostEstimate(flops=0, bytes_accessed=5 * full * width, transcendentals=0),
        name="join_grads",
    )(where, *parts)


def rotate_act_kernel(recv_ref, basis_ref, after_ref, out_ref, acts):
    @pl.when(pl.program_id(0) == 0)
    def _():
        for d in range(recv_ref.shape[0]):
            for n in range(6):
                to = n * T_SIZE + d * 16
                acts[to:to + 16, :] = recv_ref[d, n * 16:(n + 1) * 16, :]

    out_ref[...] = lax.dot_general(acts[...], basis_ref[...], NT, preferred_element_type=F32).astype(BF16)


def rotate_act(received, basis, after):
    n_dp, rows, inner = received.shape
    outer = basis.shape[0]
    return pl.pallas_call(
        rotate_act_kernel,
        grid=(outer // 256,),
        in_specs=[
            pl.BlockSpec((n_dp, rows, inner), lambda i: (0, 0, 0)),
            pl.BlockSpec((256, inner), lambda i: (i, 0)),
            TOKEN,
        ],
        out_specs=pl.BlockSpec((768, 256), lambda i: (0, i)),
        out_shape=jax.ShapeDtypeStruct((768, outer), BF16),
        scratch_shapes=[pltpu.VMEM((768, inner), BF16)],
        compiler_params=params(40),
        cost_estimate=pl.CostEstimate(flops=2 * 768 * outer * inner, bytes_accessed=6 * 1024 * 1024, transcendentals=0),
        name="rotate_act",
    )(received, basis, after)


def add_parts_kernel(parts_ref, keep_ref, came_ref, out_ref, piece_ref):
    count = parts_ref.shape[0]
    total = parts_ref[0].astype(F32)
    for s in range(1, count):
        total = total + parts_ref[s].astype(F32)
    total = total.astype(BF16)
    for s in range(count):
        out_ref[s] = total
    piece_ref[...] = (keep_ref[...].astype(F32) + came_ref[...].astype(F32)).astype(BF16)


def add_parts(parts, keep, came):
    count, rows, width = parts.shape
    high, wide = keep.shape
    return pl.pallas_call(
        add_parts_kernel,
        grid=(2,),
        in_specs=[
            pl.BlockSpec((count, rows, width // 2), lambda i: (0, 0, i)),
            pl.BlockSpec((high, wide // 2), lambda i: (0, i)),
            pl.BlockSpec((high, wide // 2), lambda i: (0, i)),
        ],
        out_specs=[
            pl.BlockSpec((count, rows, width // 2), lambda i: (0, 0, i)),
            pl.BlockSpec((high, wide // 2), lambda i: (0, i)),
        ],
        out_shape=[jax.ShapeDtypeStruct(parts.shape, BF16), jax.ShapeDtypeStruct(keep.shape, BF16)],
        compiler_params=params(40),
        cost_estimate=pl.CostEstimate(flops=parts.size, bytes_accessed=4 * parts.size, transcendentals=0),
        name="add_parts",
    )(parts, keep, came)


def query_rows_kernel(acts_ref, after_ref, out_ref):
    out_ref[...] = acts_ref[...]


def query_rows(acts, after):
    rows, width = 256, acts.shape[1]
    return pl.pallas_call(
        query_rows_kernel,
        grid=(2,),
        in_specs=[pl.BlockSpec((rows // 2, width), lambda i: (i, 0)), TOKEN],
        out_specs=pl.BlockSpec((rows // 2, width), lambda i: (i, 0)),
        out_shape=jax.ShapeDtypeStruct((rows, width), BF16),
        compiler_params=params(40),
        cost_estimate=pl.CostEstimate(flops=0, bytes_accessed=4 * rows * width, transcendentals=0),
        name="query_rows",
    )(acts, after)


PIECE = 64


def scores_kernel(core_ref, g_ref, go_ref, a_ref, ao_ref, eig_ref, out_ref, left, right):
    eigen, width = eig_ref.shape

    def tile(grads, acts, rows, n):
        part = slice(n * T_SIZE, (n + 1) * T_SIZE)
        return jnp.dot(grads[rows, part], acts[part, :], preferred_element_type=F32)

    for c in range(eigen // PIECE):
        rows = slice(c * PIECE, (c + 1) * PIECE)
        columns = slice(c * width, (c + 1) * width)
        inverse = 1.0 / (eig_ref[rows, :] + DAMPING)
        for i in range(2):
            left[i * PIECE:(i + 1) * PIECE, columns] = (tile(g_ref, a_ref, rows, i) * inverse).astype(BF16)
            left[(2 + i) * PIECE:(3 + i) * PIECE, columns] = (tile(go_ref, ao_ref, rows, i) * inverse).astype(BF16)
        for j in range(4):
            right[j * PIECE:(j + 1) * PIECE, columns] = tile(g_ref, a_ref, rows, 2 + j).astype(BF16)
    product = lax.dot_general(left[...], right[...], NT, preferred_element_type=F32)
    size = product.shape[0]
    row = lax.broadcasted_iota(jnp.int32, (size, size), 0)
    column = lax.broadcasted_iota(jnp.int32, (size, size), 1)
    own = jnp.where(row % PIECE == column % PIECE, product, 0.0)
    lane = lax.broadcasted_iota(jnp.int32, (1, size), 1)
    place = lax.broadcasted_iota(jnp.int32, (8, 128), 1)
    result = jnp.zeros((8, 128), F32)
    for i in range(4):
        line = jnp.sum(own[i * PIECE:(i + 1) * PIECE, :], axis=0, keepdims=True)
        query = (i + 2 * core_ref[0]) % 4
        for j in range(4):
            value = jnp.sum(jnp.where(lane // PIECE == j, line, 0.0), axis=1, keepdims=True) * NORM
            result = result + jnp.where(place == query * 4 + j, value, 0.0)
    out_ref[...] = result


def tile_scores(core, grads, grads_other, acts, acts_other, eigenvalues):
    eigen, width = eigenvalues.shape
    operands = (grads, grads_other, acts, acts_other, eigenvalues)
    scratch = pltpu.VMEM((4 * PIECE, eigen // PIECE * width), BF16)
    grid_spec = pltpu.PrefetchScalarGridSpec(
        num_scalar_prefetch=1,
        grid=(1,),
        in_specs=[pl.BlockSpec(operand.shape, lambda i, c: (0, 0)) for operand in operands],
        out_specs=pl.BlockSpec((8, 128), lambda i, c: (0, 0)),
        scratch_shapes=[scratch, scratch],
    )
    return pl.pallas_call(
        scores_kernel,
        grid_spec=grid_spec,
        out_shape=jax.ShapeDtypeStruct((8, 128), F32),
        compiler_params=params(40),
        cost_estimate=pl.CostEstimate(flops=4 * 8 * T_SIZE * eigen * width, bytes_accessed=8 * 1024 * 1024, transcendentals=0),
        name="tile_scores",
    )(core, *operands)


def local(query_grad, query_act, buffer_grad, buffer_act, grad_basis, act_basis, eigenvalues):
    n_dp, n_shard = lax.axis_size("dp"), lax.axis_size("shard")
    n_y = n_dp // 2
    core = lax.axis_index("buffer").astype(jnp.int32)
    place = lax.axis_index("dp").astype(jnp.int32)
    where = jnp.stack([core, place // 2, place % 2])
    swap = [(0, 1), (1, 0)]
    partner = [(d, d ^ 1) for d in range(n_dp)]

    def along_y(piece, k):
        return lax.ppermute(piece, "dp", [(d, (d + 2 * k) % n_dp) for d in range(n_dp)])

    received = lax.all_to_all(pack_acts(where, query_act, buffer_act, n_dp), "dp", 0, 0, tiled=True)
    blocks = rotate_grad(where, query_grad, buffer_grad, grad_basis, n_y)
    act_part = rotate_act(received, act_basis, blocks[0])
    parts = lax.all_to_all(act_part.reshape(n_shard, -1, act_part.shape[1]), "shard", 0, 0, tiled=True)
    keep, send = add_grads(where, [blocks[0]] + [along_y(blocks[k], k) for k in range(1, n_y)])
    sums, piece = add_parts(parts, keep, lax.ppermute(send, "dp", partner))
    acts = lax.all_to_all(sums, "shard", 0, 0, tiled=True).reshape(act_part.shape)
    pair = pair_grads(where, piece, lax.ppermute(piece, "dp", partner))
    grads, grads_query = join_grads(where, [pair] + [along_y(pair, k) for k in range(1, n_y)])
    grads_other = lax.ppermute(grads_query, "buffer", swap)
    acts_other = lax.ppermute(query_rows(acts, grads_other), "buffer", swap)
    mine = tile_scores(where, grads, grads_other, acts, acts_other, eigenvalues)
    count = n_dp * n_shard
    every = lax.all_to_all(jnp.broadcast_to(mine[None, :1], (count, 1, 128)), ("shard", "dp"), 0, 0, tiled=True)
    return jnp.sum(every, axis=(0, 1))[:16].reshape(4, 4)


def solution(mesh):
    in_specs = (
        P(None, None, "dp"),
        P(None, "dp", "shard"),
        P("buffer", None, "dp"),
        P("buffer", "dp", "shard"),
        P("shard", "dp"),
        P("dp", "shard"),
        P("shard", "dp"),
    )
    out_specs = P(None, "buffer")
    return jax.shard_map(local, mesh=mesh, in_specs=in_specs, out_specs=out_specs, check_vma=False)
```

```python
import jax
import jax.numpy as jnp
from jax import lax
from jax.experimental import pallas as pl
from jax.experimental.pallas import tpu as pltpu
from jax.sharding import PartitionSpec as P

PH = 14336
Q = 8192
T_SIZE = 128
DAMPING = 0.1
NORM = 1.0 / (T_SIZE * (float(PH) * float(Q)) ** 0.5)

F32 = jnp.float32
BF16 = jnp.bfloat16
NT = (((1,), (1,)), ((), ()))


TOKEN = pl.BlockSpec((16, 128), lambda *_: (0, 0))


def params(mib):
    return pltpu.CompilerParams(vmem_limit_bytes=mib * 1024 * 1024)


def pack_acts_kernel(core_ref, qa_ref, ba_ref, out_ref):
    half = qa_ref.shape[0] * qa_ref.shape[1]
    width = qa_ref.shape[2]
    for d in range(out_ref.shape[0]):
        out_ref[d, :half, :] = qa_ref[...].reshape(half, width)
        out_ref[d, half:, :] = ba_ref[...].reshape(2 * half, width)


def pack_acts(core, query_act, buffer_act, copies):
    _, tokens, width = query_act.shape
    grid_spec = pltpu.PrefetchScalarGridSpec(
        num_scalar_prefetch=1,
        grid=(1,),
        in_specs=[
            pl.BlockSpec((2, tokens, width), lambda i, c: (c[0], 0, 0)),
            pl.BlockSpec((4, tokens, width), lambda i, c: (0, 0, 0)),
        ],
        out_specs=pl.BlockSpec((copies, 6 * tokens, width), lambda i, c: (0, 0, 0)),
    )
    return pl.pallas_call(
        pack_acts_kernel,
        grid_spec=grid_spec,
        out_shape=jax.ShapeDtypeStruct((copies, 6 * tokens, width), BF16),
        compiler_params=params(60),
        cost_estimate=pl.CostEstimate(flops=0, bytes_accessed=2 * 1024 * 1024, transcendentals=0),
        name="pack_acts",
    )(core, query_act, buffer_act)


def rotate_grad_kernel(where_ref, qg_ref, bg_ref, basis_ref, *refs):
    outs, token_ref, part = refs[:-2], refs[-2], refs[-1]
    token_ref[...] = jnp.zeros_like(token_ref)
    width = part.shape[1]
    rows = outs[0].shape[0]

    def emit(grads):
        block = grads[...].reshape(width, grads.shape[2])
        part[...] = lax.dot_general(basis_ref[...], block, NT, preferred_element_type=F32).astype(BF16)

    @pl.when(pl.program_id(0) == 0)
    def _():
        emit(qg_ref)

    @pl.when(pl.program_id(0) > 0)
    def _():
        emit(bg_ref)

    for k, out_ref in enumerate(outs):
        start = pl.multiple_of(lax.rem(where_ref[1] + k, len(outs)) * rows, 16)
        out_ref[...] = part[pl.ds(start, rows), :]


def rotate_grad(where, query_grad, buffer_grad, basis, n_y):
    outer, inner = basis.shape
    rows = outer // n_y
    grid_spec = pltpu.PrefetchScalarGridSpec(
        num_scalar_prefetch=1,
        grid=(3,),
        in_specs=[
            pl.BlockSpec((2, T_SIZE, inner), lambda i, c: (c[0], 0, 0)),
            pl.BlockSpec((2, T_SIZE, inner), lambda i, c: (jnp.maximum(i - 1, 0), 0, 0)),
            pl.BlockSpec((outer, inner), lambda i, c: (0, 0)),
        ],
        out_specs=[pl.BlockSpec((rows, 256), lambda i, c: (0, i))] * n_y + [TOKEN],
        scratch_shapes=[pltpu.VMEM((outer, 256), BF16)],
    )
    return pl.pallas_call(
        rotate_grad_kernel,
        grid_spec=grid_spec,
        out_shape=[jax.ShapeDtypeStruct((rows, 768), BF16)] * n_y + [jax.ShapeDtypeStruct((16, 128), BF16)],
        compiler_params=params(60),
        cost_estimate=pl.CostEstimate(flops=2 * 768 * outer * inner, bytes_accessed=8 * 1024 * 1024, transcendentals=0),
        name="rotate_grad",
    )(where, query_grad, buffer_grad, basis)


def add_grads_kernel(where_ref, *refs):
    parts, keep_ref, send_ref = refs[:-3], refs[-3], refs[-2]
    total = refs[-1]
    value = parts[0][...].astype(F32)
    for part in parts[1:]:
        value = value + part[...].astype(F32)
    total[...] = value.astype(BF16)
    rows = keep_ref.shape[0]
    keep_ref[...] = total[pl.ds(pl.multiple_of(where_ref[2] * rows, 16), rows), :]
    send_ref[...] = total[pl.ds(pl.multiple_of((1 - where_ref[2]) * rows, 16), rows), :]


def add_grads(where, parts):
    rows, width = parts[0].shape
    half = jax.ShapeDtypeStruct((rows // 2, width), BF16)
    grid_spec = pltpu.PrefetchScalarGridSpec(
        num_scalar_prefetch=1,
        grid=(1,),
        in_specs=[pl.BlockSpec((rows, width), lambda i, c: (0, 0))] * len(parts),
        out_specs=[pl.BlockSpec((rows // 2, width), lambda i, c: (0, 0))] * 2,
        scratch_shapes=[pltpu.VMEM((rows, width), BF16)],
    )
    return pl.pallas_call(
        add_grads_kernel,
        grid_spec=grid_spec,
        out_shape=[half, half],
        compiler_params=params(16),
        cost_estimate=pl.CostEstimate(flops=4 * rows * width, bytes_accessed=12 * rows * width, transcendentals=0),
        name="add_grads",
    )(where, *parts)


def pair_grads_kernel(where_ref, own_ref, other_ref, out_ref):
    rows = own_ref.shape[0]
    first = where_ref[2] == 0
    out_ref[:rows, :] = jnp.where(first, own_ref[...], other_ref[...])
    out_ref[rows:, :] = jnp.where(first, other_ref[...], own_ref[...])


def pair_grads(where, own, other):
    rows, width = own.shape
    grid_spec = pltpu.PrefetchScalarGridSpec(
        num_scalar_prefetch=1,
        grid=(1,),
        in_specs=[pl.BlockSpec((rows, width), lambda i, c: (0, 0))] * 2,
        out_specs=pl.BlockSpec((2 * rows, width), lambda i, c: (0, 0)),
    )
    return pl.pallas_call(
        pair_grads_kernel,
        grid_spec=grid_spec,
        out_shape=jax.ShapeDtypeStruct((2 * rows, width), BF16),
        compiler_params=params(16),
        cost_estimate=pl.CostEstimate(flops=0, bytes_accessed=8 * rows * width, transcendentals=0),
        name="pair_grads",
    )(where, own, other)


def join_grads_kernel(where_ref, *refs):
    parts, out_ref, query_ref, token_ref = refs[:-4], refs[-3], refs[-2], refs[-1]
    token_ref[...] = jnp.zeros_like(token_ref)
    rows = parts[0].shape[0]
    half = query_ref.shape[1]
    count = len(parts)
    for k, part in enumerate(parts):
        start = pl.multiple_of(lax.rem(where_ref[1] + count - k, count) * rows, 16)
        out_ref[pl.ds(start, rows), :] = part[...]
        query_ref[pl.ds(start, rows), :] = part[:, :half]


def join_grads(where, parts, after):
    rows, width = parts[0].shape
    full = rows * len(parts)
    grid_spec = pltpu.PrefetchScalarGridSpec(
        num_scalar_prefetch=1,
        grid=(1,),
        in_specs=[pl.BlockSpec((rows, width), lambda i, c: (0, 0))] * len(parts) + [TOKEN],
        out_specs=[
            pl.BlockSpec((full, width), lambda i, c: (0, 0)),
            pl.BlockSpec((full, 256), lambda i, c: (0, 0)),
            TOKEN,
        ],
    )
    return pl.pallas_call(
        join_grads_kernel,
        grid_spec=grid_spec,
        out_shape=[
            jax.ShapeDtypeStruct((full, width), BF16),
            jax.ShapeDtypeStruct((full, 256), BF16),
            jax.ShapeDtypeStruct((16, 128), BF16),
        ],
        compiler_params=params(16),
        cost_estimate=pl.CostEstimate(flops=0, bytes_accessed=5 * full * width, transcendentals=0),
        name="join_grads",
    )(where, *parts, after)


def rotate_act_kernel(recv_ref, basis_ref, after_ref, out_ref, acts):
    @pl.when(pl.program_id(0) == 0)
    def _():
        for d in range(recv_ref.shape[0]):
            for n in range(6):
                to = n * T_SIZE + d * 16
                acts[to:to + 16, :] = recv_ref[d, n * 16:(n + 1) * 16, :]

    out_ref[...] = lax.dot_general(acts[...], basis_ref[...], NT, preferred_element_type=F32).astype(BF16)


def rotate_act(received, basis, after):
    n_dp, rows, inner = received.shape
    outer = basis.shape[0]
    return pl.pallas_call(
        rotate_act_kernel,
        grid=(outer // 256,),
        in_specs=[
            pl.BlockSpec((n_dp, rows, inner), lambda i: (0, 0, 0)),
            pl.BlockSpec((256, inner), lambda i: (i, 0)),
            TOKEN,
        ],
        out_specs=pl.BlockSpec((768, 256), lambda i: (0, i)),
        out_shape=jax.ShapeDtypeStruct((768, outer), BF16),
        scratch_shapes=[pltpu.VMEM((768, inner), BF16)],
        compiler_params=params(16),
        cost_estimate=pl.CostEstimate(flops=2 * 768 * outer * inner, bytes_accessed=6 * 1024 * 1024, transcendentals=0),
        name="rotate_act",
    )(received, basis, after)


def inverse_kernel(eig_ref, out_ref):
    out_ref[...] = (1.0 / (eig_ref[...] + DAMPING)).astype(BF16)


def inverse_of(eigenvalues):
    rows, width = eigenvalues.shape
    return pl.pallas_call(
        inverse_kernel,
        grid=(4,),
        in_specs=[pl.BlockSpec((rows // 4, width), lambda i: (i, 0))],
        out_specs=pl.BlockSpec((rows // 4, width), lambda i: (i, 0)),
        out_shape=jax.ShapeDtypeStruct((rows, width), BF16),
        compiler_params=params(16),
        cost_estimate=pl.CostEstimate(flops=2 * rows * width, bytes_accessed=8 * rows * width, transcendentals=0),
        name="inverse_of",
    )(eigenvalues)


def add_parts_kernel(parts_ref, keep_ref, came_ref, out_ref, piece_ref):
    count = parts_ref.shape[0]
    total = parts_ref[0].astype(F32)
    for s in range(1, count):
        total = total + parts_ref[s].astype(F32)
    total = total.astype(BF16)
    for s in range(count):
        out_ref[s] = total
    piece_ref[...] = (keep_ref[...].astype(F32) + came_ref[...].astype(F32)).astype(BF16)


def add_parts(parts, keep, came):
    count, rows, width = parts.shape
    high, wide = keep.shape
    return pl.pallas_call(
        add_parts_kernel,
        grid=(2,),
        in_specs=[
            pl.BlockSpec((count, rows, width // 2), lambda i: (0, 0, i)),
            pl.BlockSpec((high, wide // 2), lambda i: (0, i)),
            pl.BlockSpec((high, wide // 2), lambda i: (0, i)),
        ],
        out_specs=[
            pl.BlockSpec((count, rows, width // 2), lambda i: (0, 0, i)),
            pl.BlockSpec((high, wide // 2), lambda i: (0, i)),
        ],
        out_shape=[jax.ShapeDtypeStruct(parts.shape, BF16), jax.ShapeDtypeStruct(keep.shape, BF16)],
        compiler_params=params(16),
        cost_estimate=pl.CostEstimate(flops=parts.size, bytes_accessed=4 * parts.size, transcendentals=0),
        name="add_parts",
    )(parts, keep, came)


def query_rows_kernel(acts_ref, after_ref, out_ref):
    out_ref[...] = acts_ref[...]


def query_rows(acts, after):
    rows, width = 256, acts.shape[1]
    return pl.pallas_call(
        query_rows_kernel,
        grid=(2,),
        in_specs=[pl.BlockSpec((rows // 2, width), lambda i: (i, 0)), TOKEN],
        out_specs=pl.BlockSpec((rows // 2, width), lambda i: (i, 0)),
        out_shape=jax.ShapeDtypeStruct((rows, width), BF16),
        compiler_params=params(16),
        cost_estimate=pl.CostEstimate(flops=0, bytes_accessed=4 * rows * width, transcendentals=0),
        name="query_rows",
    )(acts, after)


PIECE = 64


def scores_kernel(core_ref, g_ref, go_ref, a_ref, ao_ref, inverse_ref, out_ref, left, right):
    eigen, width = inverse_ref.shape

    def tile(grads, acts, rows, n):
        part = slice(n * T_SIZE, (n + 1) * T_SIZE)
        return jnp.dot(grads[rows, part], acts[part, :], preferred_element_type=F32)

    for c in range(eigen // PIECE):
        rows = slice(c * PIECE, (c + 1) * PIECE)
        columns = slice(c * width, (c + 1) * width)
        inverse = inverse_ref[rows, :].astype(F32)
        for i in range(2):
            left[i * PIECE:(i + 1) * PIECE, columns] = (tile(g_ref, a_ref, rows, i) * inverse).astype(BF16)
            left[(2 + i) * PIECE:(3 + i) * PIECE, columns] = (tile(go_ref, ao_ref, rows, i) * inverse).astype(BF16)
        for j in range(4):
            right[j * PIECE:(j + 1) * PIECE, columns] = tile(g_ref, a_ref, rows, 2 + j).astype(BF16)
    product = lax.dot_general(left[...], right[...], NT, preferred_element_type=F32)
    size = product.shape[0]
    row = lax.broadcasted_iota(jnp.int32, (size, size), 0)
    column = lax.broadcasted_iota(jnp.int32, (size, size), 1)
    own = jnp.where(row % PIECE == column % PIECE, product, 0.0)
    lane = lax.broadcasted_iota(jnp.int32, (1, size), 1)
    place = lax.broadcasted_iota(jnp.int32, (1, 128), 1)
    result = jnp.zeros((1, 128), F32)
    for i in range(4):
        line = jnp.sum(own[i * PIECE:(i + 1) * PIECE, :], axis=0, keepdims=True)
        query = (i + 2 * core_ref[0]) % 4
        for j in range(4):
            value = jnp.sum(jnp.where(lane // PIECE == j, line, 0.0), axis=1, keepdims=True) * NORM
            result = result + jnp.where(place == query * 4 + j, value, 0.0)
    out_ref[...] = jnp.broadcast_to(result[None], out_ref.shape)


def tile_scores(core, grads, grads_other, acts, acts_other, inverse, copies):
    eigen, width = inverse.shape
    operands = (grads, grads_other, acts, acts_other, inverse)
    scratch = pltpu.VMEM((4 * PIECE, eigen // PIECE * width), BF16)
    grid_spec = pltpu.PrefetchScalarGridSpec(
        num_scalar_prefetch=1,
        grid=(1,),
        in_specs=[pl.BlockSpec(operand.shape, lambda i, c: (0, 0)) for operand in operands],
        out_specs=pl.BlockSpec((copies, 1, 128), lambda i, c: (0, 0, 0)),
        scratch_shapes=[scratch, scratch],
    )
    return pl.pallas_call(
        scores_kernel,
        grid_spec=grid_spec,
        out_shape=jax.ShapeDtypeStruct((copies, 1, 128), F32),
        compiler_params=params(28),
        cost_estimate=pl.CostEstimate(flops=4 * 8 * T_SIZE * eigen * width, bytes_accessed=8 * 1024 * 1024, transcendentals=0),
        name="tile_scores",
    )(core, *operands)


def local(query_grad, query_act, buffer_grad, buffer_act, grad_basis, act_basis, eigenvalues):
    n_dp, n_shard = lax.axis_size("dp"), lax.axis_size("shard")
    n_y = n_dp // 2
    core = lax.axis_index("buffer").astype(jnp.int32)
    place = lax.axis_index("dp").astype(jnp.int32)
    where = jnp.stack([core, place // 2, place % 2])
    swap = [(0, 1), (1, 0)]
    partner = [(d, d ^ 1) for d in range(n_dp)]

    def along_y(piece, k):
        return lax.ppermute(piece, "dp", [(d, (d + 2 * k) % n_dp) for d in range(n_dp)])

    received = lax.all_to_all(pack_acts(where, query_act, buffer_act, n_dp), "dp", 0, 0, tiled=True)
    *blocks, token = rotate_grad(where, query_grad, buffer_grad, grad_basis, n_y)
    act_part = rotate_act(received, act_basis, token)
    parts = lax.all_to_all(act_part.reshape(n_shard, -1, act_part.shape[1]), "shard", 0, 0, tiled=True)
    keep, send = add_grads(where, [blocks[0]] + [along_y(blocks[k], k) for k in range(1, n_y)])
    sums, piece = add_parts(parts, keep, lax.ppermute(send, "dp", partner))
    acts = lax.all_to_all(sums, "shard", 0, 0, tiled=True).reshape(act_part.shape)
    pair = pair_grads(where, piece, lax.ppermute(piece, "dp", partner))
    inverse = inverse_of(eigenvalues)
    grads, grads_query, joined = join_grads(where, [pair] + [along_y(pair, k) for k in range(1, n_y)], inverse)
    grads_other = lax.ppermute(grads_query, "buffer", swap)
    acts_other = lax.ppermute(query_rows(acts, joined), "buffer", swap)
    mine = tile_scores(where, grads, grads_other, acts, acts_other, inverse, n_dp * n_shard)
    every = lax.all_to_all(mine, ("shard", "dp"), 0, 0, tiled=True)
    return jnp.sum(every, axis=(0, 1))[:16].reshape(4, 4)


def solution(mesh):
    in_specs = (
        P(None, None, "dp"),
        P(None, "dp", "shard"),
        P("buffer", None, "dp"),
        P("buffer", "dp", "shard"),
        P("shard", "dp"),
        P("dp", "shard"),
        P("shard", "dp"),
    )
    out_specs = P(None, "buffer")
    return jax.shard_map(local, mesh=mesh, in_specs=in_specs, out_specs=out_specs, check_vma=False)
```

```python
import jax
import jax.numpy as jnp
from jax import lax
from jax.experimental import pallas as pl
from jax.experimental.pallas import tpu as pltpu
from jax.sharding import PartitionSpec as P

PH = 14336
Q = 8192
T_SIZE = 128
DAMPING = 0.1
NORM = 1.0 / (T_SIZE * (float(PH) * float(Q)) ** 0.5)

F32 = jnp.float32
BF16 = jnp.bfloat16
NT = (((1,), (1,)), ((), ()))


TOKEN = pl.BlockSpec((16, 128), lambda *_: (0, 0))


def params(mib):
    return pltpu.CompilerParams(vmem_limit_bytes=mib * 1024 * 1024)


def pack_acts_kernel(core_ref, qa_ref, ba_ref, out_ref):
    half = qa_ref.shape[0] * qa_ref.shape[1]
    width = qa_ref.shape[2]
    for d in range(out_ref.shape[0]):
        out_ref[d, :half, :] = qa_ref[...].reshape(half, width)
        out_ref[d, half:, :] = ba_ref[...].reshape(2 * half, width)


def pack_acts(core, query_act, buffer_act, copies):
    _, tokens, width = query_act.shape
    grid_spec = pltpu.PrefetchScalarGridSpec(
        num_scalar_prefetch=1,
        grid=(1,),
        in_specs=[
            pl.BlockSpec((2, tokens, width), lambda i, c: (c[0], 0, 0)),
            pl.BlockSpec((4, tokens, width), lambda i, c: (0, 0, 0)),
        ],
        out_specs=pl.BlockSpec((copies, 6 * tokens, width), lambda i, c: (0, 0, 0)),
    )
    return pl.pallas_call(
        pack_acts_kernel,
        grid_spec=grid_spec,
        out_shape=jax.ShapeDtypeStruct((copies, 6 * tokens, width), BF16),
        compiler_params=params(60),
        cost_estimate=pl.CostEstimate(flops=0, bytes_accessed=2 * 1024 * 1024, transcendentals=0),
        name="pack_acts",
    )(core, query_act, buffer_act)


def rotate_grad_kernel(where_ref, qg_ref, bg_ref, basis_ref, *refs):
    outs, token_ref, part = refs[:-2], refs[-2], refs[-1]
    token_ref[...] = jnp.zeros_like(token_ref)
    width = part.shape[1]
    rows = outs[0].shape[0]

    def emit(grads):
        block = grads[...].reshape(width, grads.shape[2])
        part[...] = lax.dot_general(basis_ref[...], block, NT, preferred_element_type=F32).astype(BF16)

    @pl.when(pl.program_id(0) == 0)
    def _():
        emit(qg_ref)

    @pl.when(pl.program_id(0) > 0)
    def _():
        emit(bg_ref)

    for k, out_ref in enumerate(outs):
        start = pl.multiple_of(lax.rem(where_ref[1] + k, len(outs)) * rows, 16)
        out_ref[...] = part[pl.ds(start, rows), :]


def rotate_grad(where, query_grad, buffer_grad, basis, n_y):
    outer, inner = basis.shape
    rows = outer // n_y
    grid_spec = pltpu.PrefetchScalarGridSpec(
        num_scalar_prefetch=1,
        grid=(3,),
        in_specs=[
            pl.BlockSpec((2, T_SIZE, inner), lambda i, c: (c[0], 0, 0)),
            pl.BlockSpec((2, T_SIZE, inner), lambda i, c: (jnp.maximum(i - 1, 0), 0, 0)),
            pl.BlockSpec((outer, inner), lambda i, c: (0, 0)),
        ],
        out_specs=[pl.BlockSpec((rows, 256), lambda i, c: (0, i))] * n_y + [TOKEN],
        scratch_shapes=[pltpu.VMEM((outer, 256), BF16)],
    )
    return pl.pallas_call(
        rotate_grad_kernel,
        grid_spec=grid_spec,
        out_shape=[jax.ShapeDtypeStruct((rows, 768), BF16)] * n_y + [jax.ShapeDtypeStruct((16, 128), BF16)],
        compiler_params=params(60),
        cost_estimate=pl.CostEstimate(flops=2 * 768 * outer * inner, bytes_accessed=8 * 1024 * 1024, transcendentals=0),
        name="rotate_grad",
    )(where, query_grad, buffer_grad, basis)


def add_grads_kernel(where_ref, *refs):
    parts, keep_ref, send_ref = refs[:-3], refs[-3], refs[-2]
    total = refs[-1]
    value = parts[0][...].astype(F32)
    for part in parts[1:]:
        value = value + part[...].astype(F32)
    total[...] = value.astype(BF16)
    rows = keep_ref.shape[0]
    keep_ref[...] = total[pl.ds(pl.multiple_of(where_ref[2] * rows, 16), rows), :]
    send_ref[...] = total[pl.ds(pl.multiple_of((1 - where_ref[2]) * rows, 16), rows), :]


def add_grads(where, parts):
    rows, width = parts[0].shape
    half = jax.ShapeDtypeStruct((rows // 2, width), BF16)
    grid_spec = pltpu.PrefetchScalarGridSpec(
        num_scalar_prefetch=1,
        grid=(1,),
        in_specs=[pl.BlockSpec((rows, width), lambda i, c: (0, 0))] * len(parts),
        out_specs=[pl.BlockSpec((rows // 2, width), lambda i, c: (0, 0))] * 2,
        scratch_shapes=[pltpu.VMEM((rows, width), BF16)],
    )
    return pl.pallas_call(
        add_grads_kernel,
        grid_spec=grid_spec,
        out_shape=[half, half],
        compiler_params=params(16),
        cost_estimate=pl.CostEstimate(flops=4 * rows * width, bytes_accessed=12 * rows * width, transcendentals=0),
        name="add_grads",
    )(where, *parts)


def pair_grads_kernel(where_ref, own_ref, other_ref, out_ref):
    rows = own_ref.shape[0]
    first = where_ref[2] == 0
    out_ref[:rows, :] = jnp.where(first, own_ref[...], other_ref[...])
    out_ref[rows:, :] = jnp.where(first, other_ref[...], own_ref[...])


def pair_grads(where, own, other):
    rows, width = own.shape
    grid_spec = pltpu.PrefetchScalarGridSpec(
        num_scalar_prefetch=1,
        grid=(1,),
        in_specs=[pl.BlockSpec((rows, width), lambda i, c: (0, 0))] * 2,
        out_specs=pl.BlockSpec((2 * rows, width), lambda i, c: (0, 0)),
    )
    return pl.pallas_call(
        pair_grads_kernel,
        grid_spec=grid_spec,
        out_shape=jax.ShapeDtypeStruct((2 * rows, width), BF16),
        compiler_params=params(16),
        cost_estimate=pl.CostEstimate(flops=0, bytes_accessed=8 * rows * width, transcendentals=0),
        name="pair_grads",
    )(where, own, other)


def join_grads_kernel(where_ref, *refs):
    parts, out_ref, query_ref, token_ref = refs[:-4], refs[-3], refs[-2], refs[-1]
    token_ref[...] = jnp.zeros_like(token_ref)
    rows = parts[0].shape[0]
    half = query_ref.shape[1]
    count = len(parts)
    for k, part in enumerate(parts):
        start = pl.multiple_of(lax.rem(where_ref[1] + count - k, count) * rows, 16)
        out_ref[pl.ds(start, rows), :] = part[...]
        query_ref[pl.ds(start, rows), :] = part[:, :half]


def join_grads(where, parts, after):
    rows, width = parts[0].shape
    full = rows * len(parts)
    grid_spec = pltpu.PrefetchScalarGridSpec(
        num_scalar_prefetch=1,
        grid=(1,),
        in_specs=[pl.BlockSpec((rows, width), lambda i, c: (0, 0))] * len(parts) + [TOKEN],
        out_specs=[
            pl.BlockSpec((full, width), lambda i, c: (0, 0)),
            pl.BlockSpec((full, 256), lambda i, c: (0, 0)),
            TOKEN,
        ],
    )
    return pl.pallas_call(
        join_grads_kernel,
        grid_spec=grid_spec,
        out_shape=[
            jax.ShapeDtypeStruct((full, width), BF16),
            jax.ShapeDtypeStruct((full, 256), BF16),
            jax.ShapeDtypeStruct((16, 128), BF16),
        ],
        compiler_params=params(16),
        cost_estimate=pl.CostEstimate(flops=0, bytes_accessed=5 * full * width, transcendentals=0),
        name="join_grads",
    )(where, *parts, after)


def rotate_act_kernel(where_ref, *refs):
    pieces, basis_ref, out_ref, acts = refs[:-4], refs[-4], refs[-2], refs[-1]
    count = len(pieces)

    @pl.when(pl.program_id(0) == 0)
    def _():
        for k, piece in enumerate(pieces):
            source = lax.rem(2 * where_ref[1] + where_ref[2] + count - k, count)
            for n in range(6):
                to = pl.multiple_of(n * T_SIZE + source * 16, 16)
                acts[pl.ds(to, 16), :] = piece[n * 16:(n + 1) * 16, :]

    out_ref[...] = lax.dot_general(acts[...], basis_ref[...], NT, preferred_element_type=F32).astype(BF16)


def rotate_act(where, pieces, basis, after):
    outer, inner = basis.shape
    grid_spec = pltpu.PrefetchScalarGridSpec(
        num_scalar_prefetch=1,
        grid=(outer // 256,),
        in_specs=[pl.BlockSpec(piece.shape, lambda i, c: (0, 0)) for piece in pieces]
        + [pl.BlockSpec((256, inner), lambda i, c: (i, 0)), TOKEN],
        out_specs=pl.BlockSpec((768, 256), lambda i, c: (0, i)),
        scratch_shapes=[pltpu.VMEM((768, inner), BF16)],
    )
    return pl.pallas_call(
        rotate_act_kernel,
        grid_spec=grid_spec,
        out_shape=jax.ShapeDtypeStruct((768, outer), BF16),
        compiler_params=params(16),
        cost_estimate=pl.CostEstimate(flops=2 * 768 * outer * inner, bytes_accessed=6 * 1024 * 1024, transcendentals=0),
        name="rotate_act",
    )(where, *pieces, basis, after)


def inverse_kernel(eig_ref, out_ref):
    out_ref[...] = (1.0 / (eig_ref[...] + DAMPING)).astype(BF16)


def inverse_of(eigenvalues):
    rows, width = eigenvalues.shape
    return pl.pallas_call(
        inverse_kernel,
        grid=(4,),
        in_specs=[pl.BlockSpec((rows // 4, width), lambda i: (i, 0))],
        out_specs=pl.BlockSpec((rows // 4, width), lambda i: (i, 0)),
        out_shape=jax.ShapeDtypeStruct((rows, width), BF16),
        compiler_params=params(16),
        cost_estimate=pl.CostEstimate(flops=2 * rows * width, bytes_accessed=8 * rows * width, transcendentals=0),
        name="inverse_of",
    )(eigenvalues)


def add_parts_kernel(parts_ref, keep_ref, came_ref, out_ref, piece_ref):
    count = parts_ref.shape[0]
    total = parts_ref[0].astype(F32)
    for s in range(1, count):
        total = total + parts_ref[s].astype(F32)
    total = total.astype(BF16)
    for s in range(count):
        out_ref[s] = total
    piece_ref[...] = (keep_ref[...].astype(F32) + came_ref[...].astype(F32)).astype(BF16)


def add_parts(parts, keep, came):
    count, rows, width = parts.shape
    high, wide = keep.shape
    return pl.pallas_call(
        add_parts_kernel,
        grid=(2,),
        in_specs=[
            pl.BlockSpec((count, rows, width // 2), lambda i: (0, 0, i)),
            pl.BlockSpec((high, wide // 2), lambda i: (0, i)),
            pl.BlockSpec((high, wide // 2), lambda i: (0, i)),
        ],
        out_specs=[
            pl.BlockSpec((count, rows, width // 2), lambda i: (0, 0, i)),
            pl.BlockSpec((high, wide // 2), lambda i: (0, i)),
        ],
        out_shape=[jax.ShapeDtypeStruct(parts.shape, BF16), jax.ShapeDtypeStruct(keep.shape, BF16)],
        compiler_params=params(16),
        cost_estimate=pl.CostEstimate(flops=parts.size, bytes_accessed=4 * parts.size, transcendentals=0),
        name="add_parts",
    )(parts, keep, came)


def query_rows_kernel(acts_ref, after_ref, out_ref):
    out_ref[...] = acts_ref[...]


def query_rows(acts, after):
    rows, width = 256, acts.shape[1]
    return pl.pallas_call(
        query_rows_kernel,
        grid=(2,),
        in_specs=[pl.BlockSpec((rows // 2, width), lambda i: (i, 0)), TOKEN],
        out_specs=pl.BlockSpec((rows // 2, width), lambda i: (i, 0)),
        out_shape=jax.ShapeDtypeStruct((rows, width), BF16),
        compiler_params=params(16),
        cost_estimate=pl.CostEstimate(flops=0, bytes_accessed=4 * rows * width, transcendentals=0),
        name="query_rows",
    )(acts, after)


PIECE = 64


def scores_kernel(core_ref, g_ref, go_ref, a_ref, ao_ref, inverse_ref, out_ref, left, right):
    eigen, width = inverse_ref.shape

    def tile(grads, acts, rows, n):
        part = slice(n * T_SIZE, (n + 1) * T_SIZE)
        return jnp.dot(grads[rows, part], acts[part, :], preferred_element_type=F32)

    for c in range(eigen // PIECE):
        rows = slice(c * PIECE, (c + 1) * PIECE)
        columns = slice(c * width, (c + 1) * width)
        inverse = inverse_ref[rows, :].astype(F32)
        for i in range(2):
            left[i * PIECE:(i + 1) * PIECE, columns] = (tile(g_ref, a_ref, rows, i) * inverse).astype(BF16)
            left[(2 + i) * PIECE:(3 + i) * PIECE, columns] = (tile(go_ref, ao_ref, rows, i) * inverse).astype(BF16)
        for j in range(4):
            right[j * PIECE:(j + 1) * PIECE, columns] = tile(g_ref, a_ref, rows, 2 + j).astype(BF16)
    product = lax.dot_general(left[...], right[...], NT, preferred_element_type=F32)
    size = product.shape[0]
    row = lax.broadcasted_iota(jnp.int32, (size, size), 0)
    column = lax.broadcasted_iota(jnp.int32, (size, size), 1)
    own = jnp.where(row % PIECE == column % PIECE, product, 0.0)
    lane = lax.broadcasted_iota(jnp.int32, (1, size), 1)
    place = lax.broadcasted_iota(jnp.int32, (1, 128), 1)
    result = jnp.zeros((1, 128), F32)
    for i in range(4):
        line = jnp.sum(own[i * PIECE:(i + 1) * PIECE, :], axis=0, keepdims=True)
        query = (i + 2 * core_ref[0]) % 4
        for j in range(4):
            value = jnp.sum(jnp.where(lane // PIECE == j, line, 0.0), axis=1, keepdims=True) * NORM
            result = result + jnp.where(place == query * 4 + j, value, 0.0)
    out_ref[...] = jnp.broadcast_to(result[None], out_ref.shape)


def tile_scores(core, grads, grads_other, acts, acts_other, inverse, copies):
    eigen, width = inverse.shape
    operands = (grads, grads_other, acts, acts_other, inverse)
    scratch = pltpu.VMEM((4 * PIECE, eigen // PIECE * width), BF16)
    grid_spec = pltpu.PrefetchScalarGridSpec(
        num_scalar_prefetch=1,
        grid=(1,),
        in_specs=[pl.BlockSpec(operand.shape, lambda i, c: (0, 0)) for operand in operands],
        out_specs=pl.BlockSpec((copies, 1, 128), lambda i, c: (0, 0, 0)),
        scratch_shapes=[scratch, scratch],
    )
    return pl.pallas_call(
        scores_kernel,
        grid_spec=grid_spec,
        out_shape=jax.ShapeDtypeStruct((copies, 1, 128), F32),
        compiler_params=params(28),
        cost_estimate=pl.CostEstimate(flops=4 * 8 * T_SIZE * eigen * width, bytes_accessed=8 * 1024 * 1024, transcendentals=0),
        name="tile_scores",
    )(core, *operands)


def local(query_grad, query_act, buffer_grad, buffer_act, grad_basis, act_basis, eigenvalues):
    n_dp, n_shard = lax.axis_size("dp"), lax.axis_size("shard")
    n_y = n_dp // 2
    core = lax.axis_index("buffer").astype(jnp.int32)
    place = lax.axis_index("dp").astype(jnp.int32)
    where = jnp.stack([core, place // 2, place % 2])
    swap = [(0, 1), (1, 0)]
    partner = [(d, d ^ 1) for d in range(n_dp)]

    def along_y(piece, k):
        return lax.ppermute(piece, "dp", [(d, (d + 2 * k) % n_dp) for d in range(n_dp)])

    tokens = pack_acts(where, query_act, buffer_act, 1)[0]
    pieces = [tokens] + [
        lax.ppermute(tokens, "dp", [(d, (d + k) % n_dp) for d in range(n_dp)]) for k in range(1, n_dp)
    ]
    *blocks, token = rotate_grad(where, query_grad, buffer_grad, grad_basis, n_y)
    act_part = rotate_act(where, pieces, act_basis, token)
    parts = lax.all_to_all(act_part.reshape(n_shard, -1, act_part.shape[1]), "shard", 0, 0, tiled=True)
    keep, send = add_grads(where, [blocks[0]] + [along_y(blocks[k], k) for k in range(1, n_y)])
    sums, piece = add_parts(parts, keep, lax.ppermute(send, "dp", partner))
    acts = lax.all_to_all(sums, "shard", 0, 0, tiled=True).reshape(act_part.shape)
    pair = pair_grads(where, piece, lax.ppermute(piece, "dp", partner))
    inverse = inverse_of(eigenvalues)
    grads, grads_query, joined = join_grads(where, [pair] + [along_y(pair, k) for k in range(1, n_y)], inverse)
    grads_other = lax.ppermute(grads_query, "buffer", swap)
    acts_other = lax.ppermute(query_rows(acts, joined), "buffer", swap)
    mine = tile_scores(where, grads, grads_other, acts, acts_other, inverse, n_dp * n_shard)
    every = lax.all_to_all(mine, ("shard", "dp"), 0, 0, tiled=True)
    return jnp.sum(every, axis=(0, 1))[:16].reshape(4, 4)


def solution(mesh):
    in_specs = (
        P(None, None, "dp"),
        P(None, "dp", "shard"),
        P("buffer", None, "dp"),
        P("buffer", "dp", "shard"),
        P("shard", "dp"),
        P("dp", "shard"),
        P("shard", "dp"),
    )
    out_specs = P(None, "buffer")
    return jax.shard_map(local, mesh=mesh, in_specs=in_specs, out_specs=out_specs, check_vma=False)
```

```python
import jax
import jax.numpy as jnp
from jax import lax
from jax.experimental import pallas as pl
from jax.experimental.pallas import tpu as pltpu
from jax.sharding import PartitionSpec as P

PH = 14336
Q = 8192
T_SIZE = 128
DAMPING = 0.1
NORM = 1.0 / (T_SIZE * (float(PH) * float(Q)) ** 0.5)

F32 = jnp.float32
BF16 = jnp.bfloat16
NT = (((1,), (1,)), ((), ()))


TOKEN = pl.BlockSpec((16, 128), lambda *_: (0, 0))


def params(mib):
    return pltpu.CompilerParams(vmem_limit_bytes=mib * 1024 * 1024)


def pack_acts_kernel(core_ref, qa_ref, ba_ref, out_ref):
    half = qa_ref.shape[0] * qa_ref.shape[1]
    width = qa_ref.shape[2]
    for d in range(out_ref.shape[0]):
        out_ref[d, :half, :] = qa_ref[...].reshape(half, width)
        out_ref[d, half:, :] = ba_ref[...].reshape(2 * half, width)


def pack_acts(core, query_act, buffer_act, copies):
    _, tokens, width = query_act.shape
    grid_spec = pltpu.PrefetchScalarGridSpec(
        num_scalar_prefetch=1,
        grid=(1,),
        in_specs=[
            pl.BlockSpec((2, tokens, width), lambda i, c: (c[0], 0, 0)),
            pl.BlockSpec((4, tokens, width), lambda i, c: (0, 0, 0)),
        ],
        out_specs=pl.BlockSpec((copies, 6 * tokens, width), lambda i, c: (0, 0, 0)),
    )
    return pl.pallas_call(
        pack_acts_kernel,
        grid_spec=grid_spec,
        out_shape=jax.ShapeDtypeStruct((copies, 6 * tokens, width), BF16),
        compiler_params=params(60),
        cost_estimate=pl.CostEstimate(flops=0, bytes_accessed=2 * 1024 * 1024, transcendentals=0),
        name="pack_acts",
    )(core, query_act, buffer_act)


def rotate_grad_kernel(where_ref, qg_ref, bg_ref, basis_ref, *refs):
    outs, token_ref, part = refs[:-2], refs[-2], refs[-1]
    token_ref[...] = jnp.zeros_like(token_ref)
    width = part.shape[1]
    rows = outs[0].shape[0]

    def emit(grads):
        block = grads[...].reshape(width, grads.shape[2])
        part[...] = lax.dot_general(basis_ref[...], block, NT, preferred_element_type=F32).astype(BF16)

    @pl.when(pl.program_id(0) == 0)
    def _():
        emit(qg_ref)

    @pl.when(pl.program_id(0) > 0)
    def _():
        emit(bg_ref)

    for k, out_ref in enumerate(outs):
        start = pl.multiple_of(lax.rem(where_ref[1] + k, len(outs)) * rows, 16)
        out_ref[...] = part[pl.ds(start, rows), :]


def rotate_grad(where, query_grad, buffer_grad, basis, n_y):
    outer, inner = basis.shape
    rows = outer // n_y
    grid_spec = pltpu.PrefetchScalarGridSpec(
        num_scalar_prefetch=1,
        grid=(3,),
        in_specs=[
            pl.BlockSpec((2, T_SIZE, inner), lambda i, c: (c[0], 0, 0)),
            pl.BlockSpec((2, T_SIZE, inner), lambda i, c: (jnp.maximum(i - 1, 0), 0, 0)),
            pl.BlockSpec((outer, inner), lambda i, c: (0, 0)),
        ],
        out_specs=[pl.BlockSpec((rows, 256), lambda i, c: (0, i))] * n_y + [TOKEN],
        scratch_shapes=[pltpu.VMEM((outer, 256), BF16)],
    )
    return pl.pallas_call(
        rotate_grad_kernel,
        grid_spec=grid_spec,
        out_shape=[jax.ShapeDtypeStruct((rows, 768), BF16)] * n_y + [jax.ShapeDtypeStruct((16, 128), BF16)],
        compiler_params=params(60),
        cost_estimate=pl.CostEstimate(flops=2 * 768 * outer * inner, bytes_accessed=8 * 1024 * 1024, transcendentals=0),
        name="rotate_grad",
    )(where, query_grad, buffer_grad, basis)


def add_grads_kernel(where_ref, *refs):
    parts, keep_ref, send_ref = refs[:-3], refs[-3], refs[-2]
    total = refs[-1]
    value = parts[0][...].astype(F32)
    for part in parts[1:]:
        value = value + part[...].astype(F32)
    total[...] = value.astype(BF16)
    rows = keep_ref.shape[0]
    keep_ref[...] = total[pl.ds(pl.multiple_of(where_ref[2] * rows, 16), rows), :]
    send_ref[...] = total[pl.ds(pl.multiple_of((1 - where_ref[2]) * rows, 16), rows), :]


def add_grads(where, parts):
    rows, width = parts[0].shape
    half = jax.ShapeDtypeStruct((rows // 2, width), BF16)
    grid_spec = pltpu.PrefetchScalarGridSpec(
        num_scalar_prefetch=1,
        grid=(1,),
        in_specs=[pl.BlockSpec((rows, width), lambda i, c: (0, 0))] * len(parts),
        out_specs=[pl.BlockSpec((rows // 2, width), lambda i, c: (0, 0))] * 2,
        scratch_shapes=[pltpu.VMEM((rows, width), BF16)],
    )
    return pl.pallas_call(
        add_grads_kernel,
        grid_spec=grid_spec,
        out_shape=[half, half],
        compiler_params=params(16),
        cost_estimate=pl.CostEstimate(flops=4 * rows * width, bytes_accessed=12 * rows * width, transcendentals=0),
        name="add_grads",
    )(where, *parts)


def pair_grads_kernel(where_ref, own_ref, other_ref, out_ref):
    rows = own_ref.shape[0]
    first = where_ref[2] == 0
    out_ref[:rows, :] = jnp.where(first, own_ref[...], other_ref[...])
    out_ref[rows:, :] = jnp.where(first, other_ref[...], own_ref[...])


def pair_grads(where, own, other):
    rows, width = own.shape
    grid_spec = pltpu.PrefetchScalarGridSpec(
        num_scalar_prefetch=1,
        grid=(1,),
        in_specs=[pl.BlockSpec((rows, width), lambda i, c: (0, 0))] * 2,
        out_specs=pl.BlockSpec((2 * rows, width), lambda i, c: (0, 0)),
    )
    return pl.pallas_call(
        pair_grads_kernel,
        grid_spec=grid_spec,
        out_shape=jax.ShapeDtypeStruct((2 * rows, width), BF16),
        compiler_params=params(16),
        cost_estimate=pl.CostEstimate(flops=0, bytes_accessed=8 * rows * width, transcendentals=0),
        name="pair_grads",
    )(where, own, other)


def join_grads_kernel(where_ref, *refs):
    parts, out_ref, query_ref, token_ref = refs[:-4], refs[-3], refs[-2], refs[-1]
    token_ref[...] = jnp.zeros_like(token_ref)
    rows = parts[0].shape[0]
    half = query_ref.shape[1]
    count = len(parts)
    for k, part in enumerate(parts):
        start = pl.multiple_of(lax.rem(where_ref[1] + count - k, count) * rows, 16)
        out_ref[pl.ds(start, rows), :] = part[...]
        query_ref[pl.ds(start, rows), :] = part[:, :half]


def join_grads(where, parts, after):
    rows, width = parts[0].shape
    full = rows * len(parts)
    grid_spec = pltpu.PrefetchScalarGridSpec(
        num_scalar_prefetch=1,
        grid=(1,),
        in_specs=[pl.BlockSpec((rows, width), lambda i, c: (0, 0))] * len(parts) + [TOKEN],
        out_specs=[
            pl.BlockSpec((full, width), lambda i, c: (0, 0)),
            pl.BlockSpec((full, 256), lambda i, c: (0, 0)),
            TOKEN,
        ],
    )
    return pl.pallas_call(
        join_grads_kernel,
        grid_spec=grid_spec,
        out_shape=[
            jax.ShapeDtypeStruct((full, width), BF16),
            jax.ShapeDtypeStruct((full, 256), BF16),
            jax.ShapeDtypeStruct((16, 128), BF16),
        ],
        compiler_params=params(16),
        cost_estimate=pl.CostEstimate(flops=0, bytes_accessed=5 * full * width, transcendentals=0),
        name="join_grads",
    )(where, *parts, after)


def rotate_act_kernel(recv_ref, basis_ref, after_ref, out_ref, acts):
    @pl.when(pl.program_id(0) == 0)
    def _():
        for d in range(recv_ref.shape[0]):
            for n in range(6):
                to = n * T_SIZE + d * 16
                acts[to:to + 16, :] = recv_ref[d, n * 16:(n + 1) * 16, :]

    out_ref[...] = lax.dot_general(acts[...], basis_ref[...], NT, preferred_element_type=F32).astype(BF16)


def rotate_act(received, basis, after):
    n_dp, rows, inner = received.shape
    outer = basis.shape[0]
    return pl.pallas_call(
        rotate_act_kernel,
        grid=(outer // 512,),
        in_specs=[
            pl.BlockSpec((n_dp, rows, inner), lambda i: (0, 0, 0)),
            pl.BlockSpec((512, inner), lambda i: (i, 0)),
            TOKEN,
        ],
        out_specs=pl.BlockSpec((768, 512), lambda i: (0, i)),
        out_shape=jax.ShapeDtypeStruct((768, outer), BF16),
        scratch_shapes=[pltpu.VMEM((768, inner), BF16)],
        compiler_params=params(16),
        cost_estimate=pl.CostEstimate(flops=2 * 768 * outer * inner, bytes_accessed=6 * 1024 * 1024, transcendentals=0),
        name="rotate_act",
    )(received, basis, after)


def inverse_kernel(eig_ref, out_ref):
    out_ref[...] = (1.0 / (eig_ref[...] + DAMPING)).astype(BF16)


def inverse_of(eigenvalues):
    rows, width = eigenvalues.shape
    return pl.pallas_call(
        inverse_kernel,
        grid=(4,),
        in_specs=[pl.BlockSpec((rows // 4, width), lambda i: (i, 0))],
        out_specs=pl.BlockSpec((rows // 4, width), lambda i: (i, 0)),
        out_shape=jax.ShapeDtypeStruct((rows, width), BF16),
        compiler_params=params(16),
        cost_estimate=pl.CostEstimate(flops=2 * rows * width, bytes_accessed=8 * rows * width, transcendentals=0),
        name="inverse_of",
    )(eigenvalues)


def add_parts_kernel(parts_ref, keep_ref, came_ref, out_ref, piece_ref):
    count = parts_ref.shape[0]
    total = parts_ref[0].astype(F32)
    for s in range(1, count):
        total = total + parts_ref[s].astype(F32)
    total = total.astype(BF16)
    for s in range(count):
        out_ref[s] = total
    piece_ref[...] = (keep_ref[...].astype(F32) + came_ref[...].astype(F32)).astype(BF16)


def add_parts(parts, keep, came):
    count, rows, width = parts.shape
    high, wide = keep.shape
    return pl.pallas_call(
        add_parts_kernel,
        grid=(1,),
        in_specs=[
            pl.BlockSpec((count, rows, width), lambda i: (0, 0, i)),
            pl.BlockSpec((high, wide), lambda i: (0, i)),
            pl.BlockSpec((high, wide), lambda i: (0, i)),
        ],
        out_specs=[
            pl.BlockSpec((count, rows, width), lambda i: (0, 0, i)),
            pl.BlockSpec((high, wide), lambda i: (0, i)),
        ],
        out_shape=[jax.ShapeDtypeStruct(parts.shape, BF16), jax.ShapeDtypeStruct(keep.shape, BF16)],
        compiler_params=params(16),
        cost_estimate=pl.CostEstimate(flops=parts.size, bytes_accessed=4 * parts.size, transcendentals=0),
        name="add_parts",
    )(parts, keep, came)


def query_rows_kernel(acts_ref, after_ref, out_ref):
    out_ref[...] = acts_ref[...]


def query_rows(acts, after):
    rows, width = 256, acts.shape[1]
    return pl.pallas_call(
        query_rows_kernel,
        grid=(2,),
        in_specs=[pl.BlockSpec((rows // 2, width), lambda i: (i, 0)), TOKEN],
        out_specs=pl.BlockSpec((rows // 2, width), lambda i: (i, 0)),
        out_shape=jax.ShapeDtypeStruct((rows, width), BF16),
        compiler_params=params(16),
        cost_estimate=pl.CostEstimate(flops=0, bytes_accessed=4 * rows * width, transcendentals=0),
        name="query_rows",
    )(acts, after)


PIECE = 64


def scores_kernel(core_ref, g_ref, go_ref, a_ref, ao_ref, inverse_ref, out_ref, left, right):
    eigen, width = inverse_ref.shape

    def tile(grads, acts, rows, n):
        part = slice(n * T_SIZE, (n + 1) * T_SIZE)
        return jnp.dot(grads[rows, part], acts[part, :], preferred_element_type=F32)

    for c in range(eigen // PIECE):
        rows = slice(c * PIECE, (c + 1) * PIECE)
        columns = slice(c * width, (c + 1) * width)
        inverse = inverse_ref[rows, :].astype(F32)
        for i in range(2):
            left[i * PIECE:(i + 1) * PIECE, columns] = (tile(g_ref, a_ref, rows, i) * inverse).astype(BF16)
            left[(2 + i) * PIECE:(3 + i) * PIECE, columns] = (tile(go_ref, ao_ref, rows, i) * inverse).astype(BF16)
        for j in range(4):
            right[j * PIECE:(j + 1) * PIECE, columns] = tile(g_ref, a_ref, rows, 2 + j).astype(BF16)
    product = lax.dot_general(left[...], right[...], NT, preferred_element_type=F32)
    size = product.shape[0]
    row = lax.broadcasted_iota(jnp.int32, (size, size), 0)
    column = lax.broadcasted_iota(jnp.int32, (size, size), 1)
    own = jnp.where(row % PIECE == column % PIECE, product, 0.0)
    lane = lax.broadcasted_iota(jnp.int32, (1, size), 1)
    place = lax.broadcasted_iota(jnp.int32, (1, 128), 1)
    result = jnp.zeros((1, 128), F32)
    for i in range(4):
        line = jnp.sum(own[i * PIECE:(i + 1) * PIECE, :], axis=0, keepdims=True)
        query = (i + 2 * core_ref[0]) % 4
        for j in range(4):
            value = jnp.sum(jnp.where(lane // PIECE == j, line, 0.0), axis=1, keepdims=True) * NORM
            result = result + jnp.where(place == query * 4 + j, value, 0.0)
    out_ref[...] = jnp.broadcast_to(result[None], out_ref.shape)


def tile_scores(core, grads, grads_other, acts, acts_other, inverse, copies):
    eigen, width = inverse.shape
    operands = (grads, grads_other, acts, acts_other, inverse)
    scratch = pltpu.VMEM((4 * PIECE, eigen // PIECE * width), BF16)
    grid_spec = pltpu.PrefetchScalarGridSpec(
        num_scalar_prefetch=1,
        grid=(1,),
        in_specs=[pl.BlockSpec(operand.shape, lambda i, c: (0, 0)) for operand in operands],
        out_specs=pl.BlockSpec((copies, 1, 128), lambda i, c: (0, 0, 0)),
        scratch_shapes=[scratch, scratch],
    )
    return pl.pallas_call(
        scores_kernel,
        grid_spec=grid_spec,
        out_shape=jax.ShapeDtypeStruct((copies, 1, 128), F32),
        compiler_params=params(28),
        cost_estimate=pl.CostEstimate(flops=4 * 8 * T_SIZE * eigen * width, bytes_accessed=8 * 1024 * 1024, transcendentals=0),
        name="tile_scores",
    )(core, *operands)


def local(query_grad, query_act, buffer_grad, buffer_act, grad_basis, act_basis, eigenvalues):
    n_dp, n_shard = lax.axis_size("dp"), lax.axis_size("shard")
    n_y = n_dp // 2
    core = lax.axis_index("buffer").astype(jnp.int32)
    place = lax.axis_index("dp").astype(jnp.int32)
    where = jnp.stack([core, place // 2, place % 2])
    swap = [(0, 1), (1, 0)]
    partner = [(d, d ^ 1) for d in range(n_dp)]

    def along_y(piece, k):
        return lax.ppermute(piece, "dp", [(d, (d + 2 * k) % n_dp) for d in range(n_dp)])

    received = lax.all_to_all(pack_acts(where, query_act, buffer_act, n_dp), "dp", 0, 0, tiled=True)
    *blocks, token = rotate_grad(where, query_grad, buffer_grad, grad_basis, n_y)
    act_part = rotate_act(received, act_basis, token)
    parts = lax.all_to_all(act_part.reshape(n_shard, -1, act_part.shape[1]), "shard", 0, 0, tiled=True)
    keep, send = add_grads(where, [blocks[0]] + [along_y(blocks[k], k) for k in range(1, n_y)])
    sums, piece = add_parts(parts, keep, lax.ppermute(send, "dp", partner))
    acts = lax.all_to_all(sums, "shard", 0, 0, tiled=True).reshape(act_part.shape)
    pair = pair_grads(where, piece, lax.ppermute(piece, "dp", partner))
    inverse = inverse_of(eigenvalues)
    grads, grads_query, joined = join_grads(where, [pair] + [along_y(pair, k) for k in range(1, n_y)], inverse)
    grads_other = lax.ppermute(grads_query, "buffer", swap)
    acts_other = lax.ppermute(query_rows(acts, joined), "buffer", swap)
    mine = tile_scores(where, grads, grads_other, acts, acts_other, inverse, n_dp * n_shard)
    every = lax.all_to_all(mine, ("shard", "dp"), 0, 0, tiled=True)
    return jnp.sum(every, axis=(0, 1))[:16].reshape(4, 4)


def solution(mesh):
    in_specs = (
        P(None, None, "dp"),
        P(None, "dp", "shard"),
        P("buffer", None, "dp"),
        P("buffer", "dp", "shard"),
        P("shard", "dp"),
        P("dp", "shard"),
        P("shard", "dp"),
    )
    out_specs = P(None, "buffer")
    return jax.shard_map(local, mesh=mesh, in_specs=in_specs, out_specs=out_specs, check_vma=False)
```
